256 devices in a mesh: state: 8 (over x, core), walker: 32 (over y, z).
Axes of the slice: x: 4, y: 4, z: 8, core: 2. Of those that a mesh axis runs over, the one named last changes fastest.
Arguments:
- positions: float32 [2, 30, 16, 4096], P(None, None, None, 'walker'), may hold values from 0 to 6
- recip: int32 [2, 128], replicated, may hold values from -3 to 3
- moire_coef: float32 [128], replicated, may hold values from -0.09375 to 0.09375
- counts: int32 [4096], P('walker'), may hold values from 1 to 7
- w_first: bfloat16 [256, 16, 256], P(None, 'state'), may hold values from -0.0625 to 0.0625
- w_second: bfloat16 [256, 16, 256], P(None, 'state'), may hold values from -0.375 to 0.375
- w_heads: bfloat16 [2, 16, 256], P(None, 'state'), may hold values from -0.375 to 0.375
Outputs:
- energy_matrix: float32 [16, 16], replicated
- grad_first: float32 [256, 16, 256], P(None, 'state')
- grad_second: float32 [256, 16, 256], P(None, 'state')
- grad_heads: float32 [2, 16, 256], P(None, 'state')
The draws below stay inside these ranges and needn't reach their ends.
All inputs are finite; a program needn't handle non-finite values.
Results may differ from the reference program's by a relative error of at most 0.0046.
Values sent between devices are 32-bit elements; how exact they have to be, the bound alone decides.
No kernel may reach another device: no remote copies, remote signals or barrier semaphores. Data moves between devices by JAX's collectives and lax.ppermute only.
A program may use at most 64 MiB of HBM per device.

```python
import math
import jax
import jax.numpy as jnp
from jax import lax

K = 16
H = 256
NG = 128
NE = 30
WALKERS = 4096


def draw_counts(key, part):
    walker_index = jnp.arange(WALKERS, dtype=jnp.int32)
    ceiling = 2 + 6 * walker_index // WALKERS
    values = jax.random.randint(key, (WALKERS,), 1, ceiling).astype(jnp.int32)
    return values.at[WALKERS - 1].set(7)


def set_ends(entries, key, least, largest):
    shape = entries.shape
    spot = [jax.random.randint(jax.random.fold_in(key, axis), (), 0, shape[axis]) for axis in range(len(shape))]
    entries = entries.at[tuple(spot)].set(least)
    longest = shape.index(max(shape))
    spot[longest] = (spot[longest] + 1) % shape[longest]
    return entries.at[tuple(spot)].set(largest)


def levels(rng, shape, pieces, low, high):
    level, own = 1.0, jax.random.fold_in(rng, 6)
    for axis_at, shards_of in pieces:
        heights = jnp.exp(jax.random.uniform(jax.random.fold_in(own, axis_at), (shards_of,), jnp.float32, low / len(pieces), high / len(pieces)))
        level = level * jnp.repeat(heights, shape[axis_at] // shards_of).reshape([-1 if axis == axis_at else 1 for axis in range(len(shape))])
    return level


def normal_values(key, dims, scale, reach, split=(), kind=jnp.bfloat16):
    result = jax.random.normal(key, dims, jnp.float32) * scale
    if len(split) > 0:
        result = levels(key, dims, split, -0.22, 0.18) * result
    return jnp.clip(result, min=-reach, max=reach).astype(kind)


def setup_inputs(seed: int = 0) -> dict:
    streams_of = jax.random.split(jax.random.key(seed), 8)
    positions = jnp.clip(6.0 * jax.random.uniform(streams_of[0], (2, NE, K, WALKERS), jnp.float32) ** levels(streams_of[0], (2, NE, K, WALKERS), ((3, 32),), -0.2, 0.2), 0.0, 6.0)
    recip = set_ends(jax.random.randint(streams_of[1], (2, NG), -3, 4), jax.random.fold_in(streams_of[1], 1), -3, 3).astype(jnp.int32)
    moire_coef = normal_values(streams_of[2], (NG,), (NE * NG) ** -0.5, 0.09375, (), jnp.float32)
    counts = draw_counts(jax.random.fold_in(streams_of[7], 71), 0)
    w_first = normal_values(streams_of[4], (2 * NG, K, H), (2 * NG * NE) ** -0.5, 0.0625, ((1, 8),))
    w_second = normal_values(streams_of[5], (H, K, H), H ** -0.5, 0.375, ((1, 8),))
    w_heads = normal_values(streams_of[6], (2, K, H), H ** -0.5, 0.375, ((1, 8),))
    return {"positions": positions, "recip": recip, "moire_coef": moire_coef, "counts": counts, "w_first": w_first, "w_second": w_second, "w_heads": w_heads}


TWO_PI = 6.283185307179586
ROOT_THREE = 1.7320508075688772
HIGHEST = lax.Precision.HIGHEST


def wave_vectors(recip):
    first_index = recip[0].astype(jnp.float32)
    second_index = recip[1].astype(jnp.float32)
    return TWO_PI * first_index, TWO_PI * (2.0 * second_index - first_index) / ROOT_THREE


def config_features(positions, recip, moire_coef, block_rows):
    electrons = positions.shape[1]
    row_count = positions.shape[2] * positions.shape[3]
    coords = positions.reshape(2, electrons, row_count // block_rows, block_rows)
    wave_x, wave_y = wave_vectors(recip)

    def one_block(portion):
        phase = portion[0][:, :, None] * wave_x[None, None, :] + portion[1][:, :, None] * wave_y[None, None, :]
        cosines = jnp.sum(jnp.cos(phase), axis=0)
        sines = jnp.sum(jnp.sin(phase), axis=0)
        potential = jnp.dot(cosines, moire_coef, precision=HIGHEST)
        return jnp.concatenate([cosines, sines], axis=1).astype(jnp.bfloat16), potential

    features_bf, potential = lax.map(one_block, jnp.moveaxis(coords, 2, 0))
    return features_bf.reshape(row_count, -1), potential.reshape(row_count)


def invert(matrix):
    size = matrix.shape[0]
    inverse = jnp.broadcast_to(jnp.eye(size, dtype=jnp.float32)[:, :, None], matrix.shape)
    for pivot in range(size):
        factor = 1.0 / matrix[pivot, pivot]
        row_matrix = matrix[pivot] * factor
        row_inverse = inverse[pivot] * factor
        column = matrix[:, pivot]
        matrix = matrix - column[:, None, :] * row_matrix[None]
        inverse = inverse - column[:, None, :] * row_inverse[None]
        matrix = matrix.at[pivot].set(row_matrix)
        inverse = inverse.at[pivot].set(row_inverse)
    return inverse


def energy_terms(amp_tiles, hps_tiles, weights):
    inverse = invert(amp_tiles)
    local_energy = jnp.einsum('ijb,jkb->ikb', inverse, hps_tiles, precision=HIGHEST)
    energy_trace = jnp.trace(local_energy, axis1=0, axis2=1)
    weighted = jnp.einsum('ikb,b->ik', local_energy, weights, precision=HIGHEST)
    return inverse, local_energy, energy_trace, weighted


def cotangent_terms(inverse, local_energy, energy_trace, energy_total, total_count, weights):
    mean_energy = jnp.trace(energy_total) / total_count
    walker_share = weights / total_count
    flipped = jnp.transpose(inverse, (1, 0, 2))
    along = jnp.einsum('kib,jkb->ijb', inverse, local_energy, precision=HIGHEST)
    d_amp = walker_share * (2.0 * (energy_trace - mean_energy) * flipped - along)
    d_hps = walker_share * flipped
    return d_amp, d_hps


def reference(positions, recip, moire_coef, counts, w_first, w_second, w_heads):
    slot_count = positions.shape[2]
    walker_count = positions.shape[3]
    row_count = slot_count * walker_count
    features_bf, potential = config_features(positions, recip, moire_coef, math.gcd(row_count, 128))
    features_wide = features_bf.astype(jnp.float32)
    stacked = (jnp.moveaxis(w_first, 1, 0), jnp.moveaxis(w_second, 1, 0), jnp.moveaxis(w_heads, 1, 0))

    def hidden_layers(w_one, w_two):
        first_act = jnp.tanh(jnp.dot(features_wide, w_one.astype(jnp.float32), precision=HIGHEST))
        first_bf = first_act.astype(jnp.bfloat16)
        second_tanh = jnp.tanh(jnp.dot(first_bf.astype(jnp.float32), w_two.astype(jnp.float32), precision=HIGHEST))
        second_bf = (second_tanh + first_act).astype(jnp.bfloat16)
        return first_act, first_bf, second_tanh, second_bf

    def forward_state(params):
        w_one, w_two, w_three = params
        first_act, first_bf, second_tanh, second_bf = hidden_layers(w_one, w_two)
        return jnp.dot(w_three.astype(jnp.float32), second_bf.astype(jnp.float32).T, precision=HIGHEST)

    outputs = lax.map(forward_state, stacked)
    squashed = jnp.tanh(outputs[:, 0].reshape(slot_count, slot_count, walker_count))
    spread = 0.75 / slot_count
    amplitude = jnp.eye(slot_count, dtype=jnp.float32)[:, :, None] + spread * squashed
    potential_grid = potential.reshape(slot_count, walker_count)[None]
    local_hps = outputs[:, 1].reshape(slot_count, slot_count, walker_count) + potential_grid * amplitude
    weights = counts.astype(jnp.float32)
    inverse, local_energy, energy_trace, weighted = energy_terms(amplitude, local_hps, weights)
    total_count = jnp.sum(weights)
    energy_matrix = weighted / total_count
    d_amp, d_hps = cotangent_terms(inverse, local_energy, energy_trace, weighted, total_count, weights)
    slope = spread * (1.0 - squashed * squashed)
    cot_amp = (d_amp + d_hps * potential_grid) * slope
    cotangent = jnp.stack([cot_amp.reshape(slot_count, row_count), d_hps.reshape(slot_count, row_count)], axis=1).astype(jnp.bfloat16)

    def backward_state(inputs):
        params, cot_state = inputs
        w_one, w_two, w_three = params
        cot_wide = cot_state.astype(jnp.float32)
        first_act, first_bf, second_tanh, second_bf = hidden_layers(w_one, w_two)
        grad_three = jnp.dot(cot_wide, second_bf.astype(jnp.float32), precision=HIGHEST)
        back_two = jnp.dot(cot_wide.T, w_three.astype(jnp.float32), precision=HIGHEST)
        inner_two = (back_two * (1.0 - second_tanh * second_tanh)).astype(jnp.bfloat16)
        grad_two = jnp.dot(first_bf.astype(jnp.float32).T, inner_two.astype(jnp.float32), precision=HIGHEST)
        back_one = back_two + jnp.dot(inner_two.astype(jnp.float32), w_two.astype(jnp.float32).T, precision=HIGHEST)
        inner_one = (back_one * (1.0 - first_act * first_act)).astype(jnp.bfloat16)
        grad_one = jnp.dot(features_wide.T, inner_one.astype(jnp.float32), precision=HIGHEST)
        return grad_one, grad_two, grad_three

    grad_one, grad_two, grad_three = lax.map(backward_state, (stacked, cotangent))
    return (energy_matrix, jnp.moveaxis(grad_one, 0, 1), jnp.moveaxis(grad_two, 0, 1), jnp.moveaxis(grad_three, 0, 1))
```

```python
import jax
import jax.numpy as jnp
import numpy as np
from jax import lax
from jax.experimental import pallas as pl
from jax.experimental.pallas import tpu as pltpu
from jax.sharding import PartitionSpec as P

F32 = jnp.float32
BF16 = jnp.bfloat16
INV_ROOT_THREE = 1.0 / 1.7320508075688772
BASIS = 64
COSINES = 25
CHUNK = 256
NN = (((1,), (0,)), ((), ()))
NT = (((1,), (1,)), ((), ()))


def half_turn_polynomials():
    squares = np.linspace(0.0, 0.25, 4001)
    root = np.sqrt(squares)
    ratio = np.where(root > 0, np.sin(np.pi * root) / np.where(root > 0, root, 1.0), np.pi)
    cheb = np.polynomial.chebyshev.Chebyshev
    sine = cheb.fit(squares, ratio, 5).convert(kind=np.polynomial.Polynomial).coef
    cosine = cheb.fit(squares, np.cos(np.pi * root), 6).convert(kind=np.polynomial.Polynomial).coef
    return [float(c) for c in sine], [float(c) for c in cosine]


SIN_COEF, COS_COEF = half_turn_polynomials()


def horner(coef, at):
    total = jnp.full_like(at, coef[-1])
    for c in coef[-2::-1]:
        total = total * at + c
    return total


def turn(t):
    rest = t - jnp.round(t)
    square = rest * rest
    sine = rest * horner(SIN_COEF, square)
    cosine = horner(COS_COEF, square)
    return 1.0 - 2.0 * sine * sine, 2.0 * sine * cosine


def mul(a, b):
    return a[0] * b[0] - a[1] * b[1], a[0] * b[1] + a[1] * b[0]


def selection(recip, copies):
    count = recip.shape[1]
    key = 7 * recip[0:1, :] + recip[1:2, :]
    size = jnp.abs(key)
    row = lax.broadcasted_iota(jnp.int32, (BASIS * copies, count), 0) % BASIS
    cosine = jnp.where(row == size, 1.0, 0.0)
    sign = jnp.where(key < 0, -1.0, 1.0)
    sine = jnp.where((row == size + (COSINES - 1)) & (size > 0), sign, 0.0)
    return cosine, sine


def three_parts(value):
    high = value.astype(BF16)
    rest = value - high.astype(F32)
    middle = rest.astype(BF16)
    low = (rest - middle.astype(F32)).astype(BF16)
    return high, middle, low


def forward_kernel(pos, recip, coef, w_one, w_two, w_heads, send, potential, basis, first, second,
                   turns, sums, w_eff, w_two_t, basis_three):
    electrons, slots, walkers = pos.shape[1:]
    states = w_one.shape[0]

    def phases(e, carry):
        x, y = pos[0, e], pos[1, e]
        third = y * INV_ROOT_THREE
        turns[0, e], turns[1, e] = turn(x - third)
        turns[2, e], turns[3, e] = turn(2.0 * third)
        return carry

    lax.fori_loop(0, electrons, phases, 0, unroll=5)

    def powers(e, rows, at, upto):
        one = (turns[at, e, rows], turns[at + 1, e, rows])
        result = [one]
        for _ in range(upto - 1):
            result.append(mul(result[-1], one))
        return result

    for half in range(slots // 8):
        rows = pl.ds(half * 8, 8)

        def put(index, value, half=half):
            sums[pl.ds(half * 8 * BASIS + index, 8, stride=BASIS), :] = value

        zero = jnp.zeros((8, walkers), F32)
        for firsts in ((1, 2), (3,)):
            alone = 3 in firsts

            def add(e, totals, firsts=firsts, alone=alone, rows=rows):
                u, v = powers(e, rows, 0, 3 if alone else 2), powers(e, rows, 2, 3)
                parts = []
                for m in firsts:
                    for n in (1, 2, 3):
                        (cu, su), (cv, sv) = u[m - 1], v[n - 1]
                        parts += [cu * cv, su * sv, su * cv, cu * sv]
                if alone:
                    for p in u + v:
                        parts += list(p)
                return tuple(t + p for t, p in zip(totals, parts, strict=True))

            number = 12 * len(firsts) + (12 if alone else 0)
            totals = lax.fori_loop(0, electrons, add, (zero,) * number, unroll=2)
            for i, m in enumerate(firsts):
                for n in (1, 2, 3):
                    cc, ss, sc, cs = totals[12 * i + 4 * (n - 1) : 12 * i + 4 * n]
                    put(7 * m + n, cc - ss)
                    put(7 * m - n, cc + ss)
                    put(COSINES - 1 + 7 * m + n, sc + cs)
                    put(COSINES - 1 + 7 * m - n, sc - cs)
            if alone:
                rest = totals[12:]
                for m in (1, 2, 3):
                    put(7 * m, rest[2 * (m - 1)])
                    put(COSINES - 1 + 7 * m, rest[2 * (m - 1) + 1])
                    put(m, rest[6 + 2 * (m - 1)])
                    put(COSINES - 1 + m, rest[6 + 2 * (m - 1) + 1])
        put(0, jnp.full((8, walkers), float(electrons), F32))
        for index in range(2 * COSINES - 1, BASIS):
            put(index, zero)

    cosine, sine = selection(recip[...], 1)
    basis_coef = jnp.sum(cosine * coef[...], axis=1, keepdims=True)
    for slot in range(slots):
        tile = sums[pl.ds(slot * BASIS, BASIS), :]
        potential[pl.ds(slot, 1), :] = jnp.sum(tile * basis_coef, axis=0, keepdims=True)
        rounded = tile.astype(BF16)
        lanes = pl.ds(slot * walkers, walkers)
        basis[:, lanes] = rounded
        for copy in range(3):
            basis_three[pl.ds(copy * BASIS, BASIS), lanes] = rounded

    cosine, sine = selection(recip[...], 3)
    select = jnp.concatenate([cosine, sine], axis=1).astype(BF16)
    part = lax.broadcasted_iota(jnp.int32, (3 * BASIS, w_one.shape[2]), 0) // BASIS
    for s in range(states):
        value = lax.dot_general(select, w_one[s], NN, preferred_element_type=F32)
        high, middle, low = (p.astype(F32) for p in three_parts(value))
        value = jnp.where(part == 0, high, jnp.where(part == 1, middle, low))
        w_eff[s] = value.T.astype(BF16)
        w_two_t[s] = w_two[s].astype(F32).T.astype(BF16)

    def chunk(c, carry):
        lanes = pl.ds(pl.multiple_of(c * CHUNK, CHUNK), CHUNK)
        for s in range(states):
            pre = lax.dot_general(w_eff[s], basis_three[:, lanes], NN, preferred_element_type=F32)
            first_act = jnp.tanh(pre)
            first[s, :, lanes] = first_act
            pre = lax.dot_general(w_two_t[s], first_act.astype(BF16), NN, preferred_element_type=F32)
            second_tanh = jnp.tanh(pre)
            second[s, :, lanes] = second_tanh
            second_bf = (second_tanh + first_act).astype(BF16)
            out = lax.dot_general(w_heads[s], second_bf, NN, preferred_element_type=F32)
            for k in range(CHUNK // walkers):
                slot = c * (CHUNK // walkers) + k
                at = slice(k * walkers, (k + 1) * walkers)
                squashed = jnp.tanh(out[0:1, at])
                other = out[1:2, at]
                for d in range(send.shape[0]):
                    send[d, pl.ds(s * 2 * slots + slot, 1), :] = squashed
                    send[d, pl.ds((s * 2 + 1) * slots + slot, 1), :] = other
        return carry

    lax.fori_loop(0, slots * walkers // CHUNK, chunk, 0)


def energy_kernel(spread, gathered, potential, counts, message, d_amp, d_hps, inverse_t):
    slots, walkers = potential.shape
    weights = counts[...].astype(F32)
    column = lax.broadcasted_iota(jnp.int32, (slots, walkers), 0)
    rows = []
    for j in range(slots):
        squashed = gathered[pl.ds(j, slots, stride=2 * slots), :]
        rows.append(jnp.where(column == j, 1.0, 0.0) + spread * squashed)
    for p in range(slots):
        factor = 1.0 / rows[p][p : p + 1, :]
        pivot = jnp.where(column == p, factor, rows[p] * factor)
        for r in range(slots):
            if r != p:
                rows[r] = jnp.where(column == p, 0.0, rows[r]) - rows[r][p : p + 1, :] * pivot
        rows[p] = pivot
    for j in range(slots):
        inverse_t[j] = rows[j]
    pot = potential[...]
    energies = [jnp.zeros((slots, walkers), F32) for _ in range(slots)]
    for j in range(slots):
        squashed = gathered[pl.ds(2 * slots * j, slots), :]
        amplitude = jnp.where(column == j, 1.0, 0.0) + spread * squashed
        hps = gathered[pl.ds(2 * slots * j + slots, slots), :] + pot * amplitude
        for k in range(slots):
            energies[k] = energies[k] + rows[j] * hps[k : k + 1, :]
    trace = jnp.zeros((1, walkers), F32)
    lane = lax.broadcasted_iota(jnp.int32, (8, walkers), 1)
    note = jnp.where(lane == 2 * slots, jnp.sum(weights, axis=1, keepdims=True), 0.0)
    for k in range(slots):
        trace = trace + energies[k][k : k + 1, :]
        total = jnp.sum(energies[k] * weights, axis=1, keepdims=True)
        for half in range(slots // 8):
            note = jnp.where(lane == half * slots + k, total[half * 8 : half * 8 + 8], note)
    for d in range(message.shape[0]):
        message[d] = note
    states = d_amp.shape[0]
    for s in range(states):
        own = inverse_t[lax.axis_index("state") * states + s]
        along = jnp.zeros((slots, walkers), F32)
        for k in range(slots):
            along = along + own[k : k + 1, :] * energies[k]
        d_amp[s] = weights * (2.0 * trace * own - along)
        d_hps[s] = weights * own


def backward_kernel(spread, messages, d_amp, d_hps, send, potential, basis, first, second, w_two,
                    w_heads, out, energy, cot, w_heads_t, first_bf, inner_one, inner_two):
    states, slots, walkers = d_amp.shape
    hidden = w_two.shape[1]
    note = messages[0]
    for d in range(1, messages.shape[0]):
        note = note + messages[d]
    lane = lax.broadcasted_iota(jnp.int32, note.shape, 1)
    sub = lax.broadcasted_iota(jnp.int32, note.shape, 0)
    count = jnp.max(jnp.where((lane == 2 * slots) & (sub == 0), note, 0.0))
    share = 1.0 / jnp.full((1, walkers), count, F32)
    diagonal = jnp.zeros(note.shape, jnp.bool_)
    for half in range(slots // 8):
        diagonal = diagonal | (lane == half * (slots + 8) + sub)
    mean = jnp.sum(jnp.where(diagonal, note, 0.0)) * share
    matrix = note * share
    for half in range(slots // 8):
        energy[pl.ds(half * 8, 8), :] = matrix[:, half * slots : (half + 1) * slots]
    pot = potential[...]
    cot[...] = jnp.zeros(cot.shape, F32)
    for s in range(states):
        squashed = send[0, pl.ds(s * 2 * slots, slots), :]
        hps = d_hps[s] * share
        amp = (d_amp[s] - 2.0 * mean * d_hps[s]) * share
        amp = (amp + hps * pot) * (spread * (1.0 - squashed * squashed))
        for slot in range(slots):
            lanes = pl.ds(slot * walkers, walkers)
            cot[s, 0:1, lanes] = amp[slot : slot + 1, :]
            cot[s, 1:2, lanes] = hps[slot : slot + 1, :]
        w_heads_t[s] = w_heads[s].astype(F32).T.astype(BF16)

    def put(start, s, value):
        for half in range(hidden // 128):
            at = pl.ds(4 * start + 2 * half + s, value.shape[0], stride=4)
            out[at, :] = value[:, half * 128 : (half + 1) * 128]

    heads0 = (jnp.zeros((16, hidden), F32),) * states

    def chunk(c, heads):
        lanes = pl.ds(pl.multiple_of(c * CHUNK, CHUNK), CHUNK)
        result = []
        for s in range(states):
            cot_bf = cot[s, :, lanes].astype(BF16)
            first_act = first[s, :, lanes]
            second_tanh = second[s, :, lanes]
            second_bf = (second_tanh + first_act).astype(BF16)
            result.append(heads[s] + lax.dot_general(cot_bf, second_bf, NT, preferred_element_type=F32))
            back_two = lax.dot_general(w_heads_t[s], cot_bf, NN, preferred_element_type=F32)
            inner = (back_two * (1.0 - second_tanh * second_tanh)).astype(BF16)
            inner_two[s, :, lanes] = inner
            back_one = back_two + lax.dot_general(w_two[s], inner, NN, preferred_element_type=F32)
            inner_one[s, :, lanes] = (back_one * (1.0 - first_act * first_act)).astype(BF16)
            first_bf[s, :, lanes] = first_act.astype(BF16)
        return tuple(result)

    heads = lax.fori_loop(0, slots * walkers // CHUNK, chunk, heads0)
    for s in range(states):
        grad_two = lax.dot_general(first_bf[s], inner_two[s], NT, preferred_element_type=F32)
        put(BASIS, s, grad_two)
        grad_one = lax.dot_general(basis[...], inner_one[s], NT, preferred_element_type=F32)
        put(0, s, grad_one)
        put(2 * COSINES - 1, s, heads[s][0:2])


def expand_kernel(summed, recip, grad_first, grad_second, grad_heads):
    cosine, sine = selection(recip[...], 3)
    select = jnp.concatenate([cosine, sine], axis=1).T.astype(BF16)
    states = grad_first.shape[1]
    rows = grad_second.shape[0]
    for half in range(2):
        lanes = pl.ds(half * 128, 128)
        for s in range(states):
            value = summed[pl.ds(2 * half + s, BASIS, stride=4), :]
            parts = jnp.concatenate(three_parts(value), axis=0)
            grad_first[:, s, lanes] = lax.dot_general(select, parts, NN, preferred_element_type=F32)
            grad_second[:, s, lanes] = summed[pl.ds(4 * BASIS + 2 * half + s, rows, stride=4), :]
            grad_heads[:, s, lanes] = value[2 * COSINES - 1 : 2 * COSINES + 1]


def vmem(count):
    return [pl.BlockSpec(memory_space=pltpu.VMEM)] * count


def call(body, outs, scratch, limit, *args):
    return pl.pallas_call(
        body,
        out_shape=[jax.ShapeDtypeStruct(s, t) for s, t in outs],
        in_specs=vmem(len(args)),
        out_specs=vmem(len(outs)),
        scratch_shapes=[pltpu.VMEM(s, t) for s, t in scratch],
        compiler_params=pltpu.CompilerParams(vmem_limit_bytes=limit << 20),
    )(*args)


def shards(positions, recip, moire_coef, counts, w_first, w_second, w_heads):
    electrons, slots, walkers = positions.shape[1:]
    features, states, hidden = w_first.shape
    rows = slots * walkers
    groups, shares = lax.axis_size("state"), lax.axis_size("walker")
    spread = 0.75 / slots
    w_one = jnp.moveaxis(w_first, 1, 0)
    w_two = jnp.moveaxis(w_second, 1, 0)
    heads = jnp.pad(jnp.moveaxis(w_heads, 1, 0), ((0, 0), (0, 16 - w_heads.shape[0]), (0, 0)))
    send, potential, basis, first, second = call(
        forward_kernel,
        [((groups, 4 * slots, walkers), F32), ((slots, walkers), F32), ((BASIS, rows), BF16),
         ((states, hidden, rows), F32), ((states, hidden, rows), F32)],
        [((4, electrons, slots, walkers), F32), ((slots * BASIS, walkers), F32),
         ((states, hidden, 3 * BASIS), BF16), ((states, hidden, hidden), BF16), ((3 * BASIS, rows), BF16)],
        40, positions, recip, moire_coef[None], w_one, w_two, heads)
    gathered = lax.all_to_all(send, "state", 0, 0, tiled=True)
    def energy_body(*refs):
        energy_kernel(spread, *refs)
    message, d_amp, d_hps = call(
        energy_body,
        [((shares, 8, walkers), F32), ((states, slots, walkers), F32), ((states, slots, walkers), F32)],
        [((slots, slots, walkers), F32)],
        16, gathered.reshape(groups * 4 * slots, walkers), potential, counts[None])
    messages = lax.all_to_all(message, "walker", 0, 0, tiled=True)
    total = 4 * (BASIS + hidden)
    def backward_body(*refs):
        backward_kernel(spread, *refs)
    grads, energy_matrix = call(
        backward_body,
        [((total, 128), F32), ((slots, slots), F32)],
        [((states, 16, rows), F32), ((states, hidden, 16), BF16), ((states, hidden, rows), BF16),
         ((states, hidden, rows), BF16), ((states, hidden, rows), BF16)],
        40, messages, d_amp, d_hps, send, potential, basis, first, second, w_two, heads)
    pieces = lax.all_to_all(grads.reshape(shares, total // shares, 128), "walker", 0, 0, tiled=True)
    piece = jnp.broadcast_to(jnp.sum(pieces, axis=0)[None], pieces.shape)
    summed = lax.all_to_all(piece, "walker", 0, 0, tiled=True)
    grad_first, grad_second, grad_heads = call(
        expand_kernel,
        [(w_first.shape, F32), (w_second.shape, F32), (w_heads.shape, F32)],
        [], 16, summed.reshape(total, 128), recip)
    return (energy_matrix, grad_first, grad_second, grad_heads)


def solution(mesh):
    in_specs = (
        P(None, None, None, "walker"),
        P(),
        P(),
        P("walker"),
        P(None, "state", None),
        P(None, "state", None),
        P(None, "state", None),
    )
    out_specs = (P(), P(None, "state", None), P(None, "state", None), P(None, "state", None))
    return jax.shard_map(shards, mesh=mesh, in_specs=in_specs, out_specs=out_specs, check_vma=False)
```

```python
import jax
import jax.numpy as jnp
import numpy as np
from jax import lax
from jax.experimental import pallas as pl
from jax.experimental.pallas import tpu as pltpu
from jax.sharding import Mesh
from jax.sharding import PartitionSpec as P

F32 = jnp.float32
BF16 = jnp.bfloat16
INV_ROOT_THREE = 1.0 / 1.7320508075688772
XS, YS, ZS = 4, 4, 8
BASIS = 64
COSINES = 25
NN = (((1,), (0,)), ((), ()))
NT = (((1,), (1,)), ((), ()))


def half_turn_polynomials():
    squares = np.linspace(0.0, 0.25, 4001)
    root = np.sqrt(squares)
    ratio = np.where(root > 0, np.sin(np.pi * root) / np.where(root > 0, root, 1.0), np.pi)
    cheb = np.polynomial.chebyshev.Chebyshev
    sine = cheb.fit(squares, ratio, 5).convert(kind=np.polynomial.Polynomial).coef
    cosine = cheb.fit(squares, np.cos(np.pi * root), 6).convert(kind=np.polynomial.Polynomial).coef
    return [float(c) for c in sine], [float(c) for c in cosine]


SIN_COEF, COS_COEF = half_turn_polynomials()


def horner(coef, at):
    total = jnp.full_like(at, coef[-1])
    for c in coef[-2::-1]:
        total = total * at + c
    return total


def turn(t):
    rest = t - jnp.round(t)
    square = rest * rest
    sine = rest * horner(SIN_COEF, square)
    cosine = horner(COS_COEF, square)
    return 1.0 - 2.0 * sine * sine, 2.0 * sine * cosine


def mul(a, b):
    return a[0] * b[0] - a[1] * b[1], a[0] * b[1] + a[1] * b[0]


def selection(recip, copies):
    count = recip.shape[1]
    key = 7 * recip[0:1, :] + recip[1:2, :]
    size = jnp.abs(key)
    row = lax.broadcasted_iota(jnp.int32, (BASIS * copies, count), 0) % BASIS
    cosine = jnp.where(row == size, 1.0, 0.0)
    sign = jnp.where(key < 0, -1.0, 1.0)
    sine = jnp.where((row == size + (COSINES - 1)) & (size > 0), sign, 0.0)
    return cosine, sine


def three_parts(value):
    high = value.astype(BF16)
    rest = value - high.astype(F32)
    middle = rest.astype(BF16)
    low = (rest - middle.astype(F32)).astype(BF16)
    return high, middle, low


def forward_kernel(pos_in, recip_in, coef_in, counts_in, w_one_in, w_two_in, w_heads_in,
                   send, potential, basis, first, second, weights, select_out, w_two, w_heads_t,
                   pos, recip, coef, counts, w_one_raw, w_two_raw, w_heads_raw, arrived,
                   turns, sums, w_eff, w_two_t, basis_three):
    electrons, slots, walkers = pos.shape[1:]
    states = w_two.shape[0]
    copies = []
    for source, target in ((pos_in, pos), (recip_in, recip), (coef_in, coef), (counts_in, counts),
                           (w_one_in, w_one_raw), (w_two_in, w_two_raw), (w_heads_in, w_heads_raw)):
        copies.append(pltpu.make_async_copy(source, target, arrived.at[len(copies)]))
        copies[-1].start()
    copies[0].wait()

    def phases(e, carry):
        x, y = pos[0, e], pos[1, e]
        third = y * INV_ROOT_THREE
        turns[0, e], turns[1, e] = turn(x - third)
        turns[2, e], turns[3, e] = turn(2.0 * third)
        return carry

    lax.fori_loop(0, electrons, phases, 0, unroll=5)

    def powers(e, rows, at, upto):
        one = (turns[at, e, rows], turns[at + 1, e, rows])
        result = [one]
        for _ in range(upto - 1):
            result.append(mul(result[-1], one))
        return result

    for half in range(slots // 8):
        rows = pl.ds(half * 8, 8)

        def put(index, value, half=half):
            sums[pl.ds(half * 8 * BASIS + index, 8, stride=BASIS), :] = value

        zero = jnp.zeros((8, walkers), F32)
        for firsts in ((1, 2), (3,)):
            alone = 3 in firsts

            def add(e, totals, firsts=firsts, alone=alone, rows=rows):
                u, v = powers(e, rows, 0, 3 if alone else 2), powers(e, rows, 2, 3)
                parts = []
                for m in firsts:
                    for n in (1, 2, 3):
                        (cu, su), (cv, sv) = u[m - 1], v[n - 1]
                        parts += [cu * cv, su * sv, su * cv, cu * sv]
                if alone:
                    for p in u + v:
                        parts += list(p)
                return tuple(t + p for t, p in zip(totals, parts, strict=True))

            number = 12 * len(firsts) + (12 if alone else 0)
            totals = lax.fori_loop(0, electrons, add, (zero,) * number, unroll=2)
            for i, m in enumerate(firsts):
                for n in (1, 2, 3):
                    cc, ss, sc, cs = totals[12 * i + 4 * (n - 1) : 12 * i + 4 * n]
                    put(7 * m + n, cc - ss)
                    put(7 * m - n, cc + ss)
                    put(COSINES - 1 + 7 * m + n, sc + cs)
                    put(COSINES - 1 + 7 * m - n, sc - cs)
            if alone:
                rest = totals[12:]
                for m in (1, 2, 3):
                    put(7 * m, rest[2 * (m - 1)])
                    put(COSINES - 1 + 7 * m, rest[2 * (m - 1) + 1])
                    put(m, rest[6 + 2 * (m - 1)])
                    put(COSINES - 1 + m, rest[6 + 2 * (m - 1) + 1])
        put(0, jnp.full((8, walkers), float(electrons), F32))
        for index in range(2 * COSINES - 1, BASIS):
            put(index, zero)

    for copy in copies[1:]:
        copy.wait()
    weights[...] = counts[...].astype(F32)
    cosine, sine = selection(recip[...], 1)
    basis_coef = jnp.sum(cosine * coef[...], axis=1, keepdims=True)
    for slot in range(slots):
        tile = sums[pl.ds(slot * BASIS, BASIS), :]
        potential[pl.ds(slot, 1), :] = jnp.sum(tile * basis_coef, axis=0, keepdims=True)
        rounded = tile.astype(BF16)
        lanes = pl.ds(slot * walkers, walkers)
        basis[:, lanes] = rounded
        for copy in range(3):
            basis_three[pl.ds(copy * BASIS, BASIS), lanes] = rounded

    cosine, sine = selection(recip[...], 3)
    select = jnp.concatenate([cosine, sine], axis=1)
    select_out[...] = select.T.astype(BF16)
    select = select.astype(BF16)
    part = lax.broadcasted_iota(jnp.int32, (3 * BASIS, w_two.shape[2]), 0) // BASIS
    heads = []
    for s in range(states):
        value = lax.dot_general(select, w_one_raw[:, s, :], NN, preferred_element_type=F32)
        high, middle, low = (p.astype(F32) for p in three_parts(value))
        value = jnp.where(part == 0, high, jnp.where(part == 1, middle, low))
        w_eff[s] = value.T.astype(BF16)
        value = w_two_raw[:, s, :]
        w_two[s] = value
        w_two_t[s] = value.astype(F32).T.astype(BF16)
        value = w_heads_raw[:, s, :].astype(F32)
        value = jnp.concatenate([value, jnp.zeros((16 - value.shape[0], value.shape[1]), F32)], axis=0)
        heads.append(value.astype(BF16))
        w_heads_t[s, 0] = value.T.astype(BF16)
        value = jnp.concatenate([jnp.zeros((2, value.shape[1]), F32), value[0:1], jnp.zeros((13, value.shape[1]), F32)], axis=0)
        w_heads_t[s, 1] = value.T.astype(BF16)

    for s in range(states):
        pre = lax.dot_general(w_eff[s], basis_three[...], NN, preferred_element_type=F32)
        first_act = jnp.tanh(pre)
        first[s] = first_act
        pre = lax.dot_general(w_two_t[s], first_act.astype(BF16), NN, preferred_element_type=F32)
        second_tanh = jnp.tanh(pre)
        second[s] = second_tanh
        second_bf = (second_tanh + first_act).astype(BF16)
        out = lax.dot_general(heads[s], second_bf, NN, preferred_element_type=F32)
        for slot in range(slots):
            at = slice(slot * walkers, (slot + 1) * walkers)
            send[pl.ds(s * 2 * slots + slot, 1), :] = jnp.tanh(out[0:1, at])
            send[pl.ds((s * 2 + 1) * slots + slot, 1), :] = out[1:2, at]


def invert_transposed(spread, gathered, slots, walkers):
    column = lax.broadcasted_iota(jnp.int32, (slots, walkers), 0)
    rows = []
    for j in range(slots):
        squashed = gathered[pl.ds(j, slots, stride=2 * slots), :]
        rows.append(jnp.where(column == j, 1.0, 0.0) + spread * squashed)
    for p in range(slots):
        factor = 1.0 / rows[p][p : p + 1, :]
        pivot = jnp.where(column == p, factor, rows[p] * factor)
        for r in range(slots):
            if r != p:
                rows[r] = jnp.where(column == p, 0.0, rows[r]) - rows[r][p : p + 1, :] * pivot
        rows[p] = pivot
    return rows


def backward_kernel(spread, *refs):
    along_x, refs = refs[:XS], refs[XS:]
    others, potential, weights_in, basis, first, second, w_two, w_heads_t = refs[:8]
    outs, (gathered, inverse_t, value, slope, cot, first_bf, inner_one, inner_two) = refs[8 : 8 + YS], refs[8 + YS :]
    send = along_x[0]
    slots, walkers = potential.shape
    states, hidden = w_two.shape[:2]
    rows_number = slots * walkers
    block = send.shape[0]
    me_x, me_core = lax.axis_index("x"), lax.axis_index("core")
    for k in range(XS):
        for at, source in ((me_core, along_x[k]), (1 - me_core, others.at[k])):
            owner = (me_x + XS - k) % XS * 2 + at
            gathered[pl.ds(pl.multiple_of(owner * block, block), block), :] = source[...]

    weights = weights_in[...]
    rows = invert_transposed(spread, gathered, slots, walkers)
    for j in range(slots):
        inverse_t[j] = rows[j]
    pot = potential[...]
    column = lax.broadcasted_iota(jnp.int32, (slots, walkers), 0)
    energies = [jnp.zeros((slots, walkers), F32) for _ in range(slots)]
    for j in range(slots):
        squashed = gathered[pl.ds(2 * slots * j, slots), :]
        amplitude = jnp.where(column == j, 1.0, 0.0) + spread * squashed
        hps = gathered[pl.ds(2 * slots * j + slots, slots), :] + pot * amplitude
        for k in range(slots):
            energies[k] = energies[k] + rows[j] * hps[k : k + 1, :]
    trace = jnp.zeros((1, walkers), F32)
    lane = lax.broadcasted_iota(jnp.int32, (8, walkers), 1)
    sums = jnp.zeros((8, walkers), F32)
    for k in range(slots):
        trace = trace + energies[k][k : k + 1, :]
        total = jnp.sum(energies[k] * weights, axis=1, keepdims=True)
        for half in range(slots // 8):
            sums = jnp.where(lane == half * slots + k, total[half * 8 : half * 8 + 8], sums)
    count = jnp.sum(weights, axis=1, keepdims=True)
    level = jnp.sum(trace * weights, axis=1, keepdims=True)
    center = level / count
    note = jnp.where(lane == 0, level, jnp.where(lane == 1, count, 0.0))

    cot[...] = jnp.zeros(cot.shape, F32)
    for s in range(states):
        own = inverse_t[(me_x * 2 + me_core) * states + s]
        along_own = jnp.zeros((slots, walkers), F32)
        for k in range(slots):
            along_own = along_own + own[k : k + 1, :] * energies[k]
        hps = weights * own
        amp = weights * (2.0 * (trace - center) * own - along_own)
        squashed = send[pl.ds(s * 2 * slots, slots), :]
        bend = spread * (1.0 - squashed * squashed)
        amp = (amp + hps * pot) * bend
        steep = -2.0 * hps * bend
        for slot in range(slots):
            lanes = pl.ds(slot * walkers, walkers)
            cot[s, 0:1, lanes] = amp[slot : slot + 1, :]
            cot[s, 1:2, lanes] = hps[slot : slot + 1, :]
            cot[s, 2:3, lanes] = steep[slot : slot + 1, :]

    def put(target, start, s, array):
        for half in range(hidden // 128):
            at = pl.ds(4 * start + 2 * half + s, array.shape[0], stride=4)
            target[at, :] = array[:, half * 128 : (half + 1) * 128]

    heads = []
    for s in range(states):
        first_act = first[s]
        second_tanh = second[s]
        second_bf = (second_tanh + first_act).astype(BF16)
        first_bf[s] = first_act.astype(BF16)
        bend_one = 1.0 - first_act * first_act
        bend_two = 1.0 - second_tanh * second_tanh
        cot_bf = cot[s].astype(BF16)
        heads.append(lax.dot_general(cot_bf, second_bf, NT, preferred_element_type=F32))
        for t in range(2):
            back_two = lax.dot_general(w_heads_t[s, t], cot_bf, NN, preferred_element_type=F32)
            inner = (back_two * bend_two).astype(BF16)
            inner_two[s, t] = inner
            back_one = back_two + lax.dot_general(w_two[s], inner, NN, preferred_element_type=F32)
            inner_one[s, t] = (back_one * bend_one).astype(BF16)
    for t, target in enumerate((value, slope)):
        spare = 4 * (2 * COSINES - 1)
        target[pl.ds(spare, 4 * BASIS - spare), :] = jnp.zeros((4 * BASIS - spare, 128), F32)
        for s in range(states):
            grad_two = lax.dot_general(first_bf[s], inner_two[s, t], NT, preferred_element_type=F32)
            put(target, BASIS, s, grad_two)
            grad_one = lax.dot_general(basis[...], inner_one[s, t], NT, preferred_element_type=F32)
            put(target, 0, s, grad_one[0 : 2 * COSINES - 1])
            put(target, 2 * COSINES - 1, s, heads[s][2 * t : 2 * t + 2])
    value[pl.ds(4 * (2 * COSINES + 1), 8), :] = sums
    part = value.shape[0] // YS
    y = lax.axis_index("y")
    for k in range(YS):
        at = pl.ds(pl.multiple_of((y + k) % YS * part, part), part)
        outs[k][pl.ds(0, part), :] = value[at, :] - center * slope[at, :]
        outs[k][pl.ds(part, part), :] = slope[at, :]
        outs[k][pl.ds(2 * part, 8), :] = note


def line_kernel(*refs):
    parts, out = refs[:YS], refs[YS]
    part = (parts[0].shape[0] - 8) // 2
    size = part // ZS

    def added(start, length):
        total = parts[0][pl.ds(start, length), :]
        for k in range(1, YS):
            total = total + parts[k][pl.ds(start, length), :]
        return total

    for z in range(ZS):
        out[z, 0:size] = added(z * size, size)
        out[z, size : 2 * size] = added(part + z * size, size)
        out[z, 2 * size : 2 * size + 8] = added(2 * part, 8)


def piece_kernel(parts, out):
    size = out.shape[1]
    total = parts[0]
    for z in range(1, ZS):
        total = total + parts[z]
    note = total[2 * size : 2 * size + 1]
    share = 1.0 / note[:, 1:2]
    mean = note[:, 0:1] * share
    piece = (total[0:size] + mean * total[size : 2 * size]) * share
    for z in range(ZS):
        out[z] = piece


def expand_kernel(*refs):
    parts, (select_in, energy, grad_first, grad_second, grad_heads, summed) = refs[:YS], refs[YS:]
    y = lax.axis_index("y")
    part = parts[0].shape[0]
    for k in range(YS):
        summed[pl.ds(pl.multiple_of((y + YS - k) % YS * part, part), part), :] = parts[k][...]
    select = select_in[...]
    slots = energy.shape[0]
    note = summed[pl.ds(4 * (2 * COSINES + 1), 8), :]
    for half in range(slots // 8):
        energy[pl.ds(half * 8, 8), :] = note[:, half * slots : (half + 1) * slots]
    states = grad_first.shape[1]
    rows = grad_second.shape[0]
    for half in range(2):
        lanes = pl.ds(half * 128, 128)
        for s in range(states):
            value = summed[pl.ds(2 * half + s, BASIS, stride=4), :]
            parts = jnp.concatenate(three_parts(value), axis=0)
            grad_first[:, s, lanes] = lax.dot_general(select, parts, NN, preferred_element_type=F32)
            grad_second[:, s, lanes] = summed[pl.ds(4 * BASIS + 2 * half + s, rows, stride=4), :]
            grad_heads[:, s, lanes] = value[2 * COSINES - 1 : 2 * COSINES + 1]


def call(body, outs, scratch, limit, args, flops, hbm=False):
    place = pltpu.HBM if hbm else pltpu.VMEM
    if hbm:
        args = [pltpu.with_memory_space_constraint(a, pltpu.HBM) for a in args]
    return pl.pallas_call(
        body,
        out_shape=[jax.ShapeDtypeStruct(s, t) for s, t in outs],
        in_specs=[pl.BlockSpec(memory_space=place)] * len(args),
        out_specs=[pl.BlockSpec(memory_space=pltpu.VMEM)] * len(outs),
        scratch_shapes=[pltpu.VMEM(*s) if isinstance(s, tuple) else s for s in scratch],
        compiler_params=pltpu.CompilerParams(vmem_limit_bytes=limit << 20),
        cost_estimate=pl.CostEstimate(flops=flops, bytes_accessed=1 << 20, transcendentals=0),
    )(*args)


def along(axis, array, shift):
    size = lax.axis_size(axis)
    return lax.ppermute(array, axis, [(d, (d + shift) % size) for d in range(size)])


def shards(positions, recip, moire_coef, counts, w_first, w_second, w_heads):
    electrons, slots, walkers = positions.shape[1:]
    features, states, hidden = w_first.shape
    rows = slots * walkers
    groups = lax.axis_size(("x", "core"))
    spread = 0.75 / slots
    total = 4 * (BASIS + hidden)
    work = 2 * states * rows * hidden * hidden
    args = (positions, recip, moire_coef[None], counts[None], w_first, w_second, w_heads)
    send, potential, basis, first, second, weights, select, w_two, w_heads_t = call(
        forward_kernel,
        [((4 * slots, walkers), F32), ((slots, walkers), F32), ((BASIS, rows), BF16),
         ((states, hidden, rows), F32), ((states, hidden, rows), F32), ((1, walkers), F32),
         ((features, 3 * BASIS), BF16), ((states, hidden, hidden), BF16), ((states, 2, hidden, 16), BF16)],
        [(a.shape, a.dtype) for a in args] + [pltpu.SemaphoreType.DMA((len(args),))]
        + [((4, electrons, slots, walkers), F32), ((slots * BASIS, walkers), F32),
           ((states, hidden, 3 * BASIS), BF16), ((states, hidden, hidden), BF16), ((3 * BASIS, rows), BF16)],
        40, args, 2 * work, hbm=True)
    along_x = [send] + [along("x", send, k) for k in range(1, XS)]
    others = along("core", jnp.stack(along_x), 1)

    def backward_body(*refs):
        backward_kernel(spread, *refs)

    part = total // YS
    size = part // ZS
    parts = call(
        backward_body,
        [((2 * part + 8, 128), F32)] * YS,
        [((groups * 4 * slots, walkers), F32), ((slots, slots, walkers), F32), ((total, 128), F32),
         ((total, 128), F32), ((states, 16, rows), F32), ((states, hidden, rows), BF16),
         ((states, 2, hidden, rows), BF16), ((states, 2, hidden, rows), BF16)],
        24, (*along_x, others, potential, weights, basis, first, second, w_two, w_heads_t), 6 * work)
    parts = [parts[0]] + [along("y", parts[k], k) for k in range(1, YS)]
    lines, = call(line_kernel, [((ZS, 2 * size + 8, 128), F32)], [], 4, parts, 1 << 20)
    lines = lax.all_to_all(lines, "z", 0, 0, tiled=True)
    pieces, = call(piece_kernel, [((ZS, size, 128), F32)], [], 4, (lines,), 1 << 20)
    summed = lax.all_to_all(pieces, "z", 0, 0, tiled=True).reshape(part, 128)
    parts = [summed] + [along("y", summed, k) for k in range(1, YS)]
    return call(
        expand_kernel,
        [((slots, slots), F32), (w_first.shape, F32), (w_second.shape, F32), (w_heads.shape, F32)],
        [((total, 128), F32)], 8, (*parts, select), 1 << 20)


def solution(mesh):
    mesh = Mesh(mesh.devices.reshape(XS, 2, YS, ZS), ("x", "core", "y", "z"))
    state, walker = ("x", "core"), ("y", "z")
    in_specs = (
        P(None, None, None, walker),
        P(),
        P(),
        P(walker),
        P(None, state, None),
        P(None, state, None),
        P(None, state, None),
    )
    out_specs = (P(), P(None, state, None), P(None, state, None), P(None, state, None))
    return jax.shard_map(shards, mesh=mesh, in_specs=in_specs, out_specs=out_specs, check_vma=False)
```

```python
import jax
import jax.numpy as jnp
import numpy as np
from jax import lax
from jax.experimental import pallas as pl
from jax.experimental.pallas import tpu as pltpu
from jax.sharding import Mesh
from jax.sharding import PartitionSpec as P

F32 = jnp.float32
BF16 = jnp.bfloat16
INV_ROOT_THREE = 1.0 / 1.7320508075688772
XS, YS, ZS = 4, 4, 8
BASIS = 64
COSINES = 25
NN = (((1,), (0,)), ((), ()))
NT = (((1,), (1,)), ((), ()))


def half_turn_polynomials():
    squares = np.linspace(0.0, 0.25, 4001)
    root = np.sqrt(squares)
    ratio = np.where(root > 0, np.sin(np.pi * root) / np.where(root > 0, root, 1.0), np.pi)
    cheb = np.polynomial.chebyshev.Chebyshev
    sine = cheb.fit(squares, ratio, 5).convert(kind=np.polynomial.Polynomial).coef
    cosine = cheb.fit(squares, np.cos(np.pi * root), 6).convert(kind=np.polynomial.Polynomial).coef
    return [float(c) for c in sine], [float(c) for c in cosine]


SIN_COEF, COS_COEF = half_turn_polynomials()


def horner(coef, at):
    total = jnp.full_like(at, coef[-1])
    for c in coef[-2::-1]:
        total = total * at + c
    return total


def turn(t):
    rest = t - jnp.round(t)
    square = rest * rest
    sine = rest * horner(SIN_COEF, square)
    cosine = horner(COS_COEF, square)
    return 1.0 - 2.0 * sine * sine, 2.0 * sine * cosine


def mul(a, b):
    return a[0] * b[0] - a[1] * b[1], a[0] * b[1] + a[1] * b[0]


def selection(recip, copies):
    count = recip.shape[1]
    key = 7 * recip[0:1, :] + recip[1:2, :]
    size = jnp.abs(key)
    row = lax.broadcasted_iota(jnp.int32, (BASIS * copies, count), 0) % BASIS
    cosine = jnp.where(row == size, 1.0, 0.0)
    sign = jnp.where(key < 0, -1.0, 1.0)
    sine = jnp.where((row == size + (COSINES - 1)) & (size > 0), sign, 0.0)
    return cosine, sine


def three_parts(value):
    high = value.astype(BF16)
    rest = value - high.astype(F32)
    middle = rest.astype(BF16)
    low = (rest - middle.astype(F32)).astype(BF16)
    return high, middle, low


def forward_kernel(pos_in, recip_in, coef_in, counts_in, w_one_in, w_two_in, w_heads_in,
                   send, potential, basis, first, second, weights, select_out, w_two, w_heads_t,
                   pos, recip, coef, counts, w_one_raw, w_two_raw, w_heads_raw, arrived,
                   turns, sums, w_eff, w_two_t, basis_three):
    electrons, slots, walkers = pos.shape[1:]
    states = w_two.shape[0]
    copies = []
    for source, target in ((pos_in, pos), (recip_in, recip), (coef_in, coef), (counts_in, counts),
                           (w_one_in, w_one_raw), (w_two_in, w_two_raw), (w_heads_in, w_heads_raw)):
        copies.append(pltpu.make_async_copy(source, target, arrived.at[len(copies)]))
        copies[-1].start()
    copies[0].wait()

    def phases(e, carry):
        x, y = pos[0, e], pos[1, e]
        third = y * INV_ROOT_THREE
        turns[0, e], turns[1, e] = turn(x - third)
        turns[2, e], turns[3, e] = turn(2.0 * third)
        return carry

    lax.fori_loop(0, electrons, phases, 0, unroll=5)

    def powers(e, rows, at, upto):
        one = (turns[at, e, rows], turns[at + 1, e, rows])
        result = [one]
        for _ in range(upto - 1):
            result.append(mul(result[-1], one))
        return result

    for half in range(slots // 8):
        rows = pl.ds(half * 8, 8)

        def put(index, value, half=half):
            sums[pl.ds(half * 8 * BASIS + index, 8, stride=BASIS), :] = value

        zero = jnp.zeros((8, walkers), F32)
        for firsts in ((1, 2), (3,)):
            alone = 3 in firsts

            def add(e, totals, firsts=firsts, alone=alone, rows=rows):
                u, v = powers(e, rows, 0, 3 if alone else 2), powers(e, rows, 2, 3)
                parts = []
                for m in firsts:
                    for n in (1, 2, 3):
                        (cu, su), (cv, sv) = u[m - 1], v[n - 1]
                        parts += [cu * cv, su * sv, su * cv, cu * sv]
                if alone:
                    for p in u + v:
                        parts += list(p)
                return tuple(t + p for t, p in zip(totals, parts, strict=True))

            number = 12 * len(firsts) + (12 if alone else 0)
            totals = lax.fori_loop(0, electrons, add, (zero,) * number, unroll=2)
            for i, m in enumerate(firsts):
                for n in (1, 2, 3):
                    cc, ss, sc, cs = totals[12 * i + 4 * (n - 1) : 12 * i + 4 * n]
                    put(7 * m + n, cc - ss)
                    put(7 * m - n, cc + ss)
                    put(COSINES - 1 + 7 * m + n, sc + cs)
                    put(COSINES - 1 + 7 * m - n, sc - cs)
            if alone:
                rest = totals[12:]
                for m in (1, 2, 3):
                    put(7 * m, rest[2 * (m - 1)])
                    put(COSINES - 1 + 7 * m, rest[2 * (m - 1) + 1])
                    put(m, rest[6 + 2 * (m - 1)])
                    put(COSINES - 1 + m, rest[6 + 2 * (m - 1) + 1])
        put(0, jnp.full((8, walkers), float(electrons), F32))
        for index in range(2 * COSINES - 1, BASIS):
            put(index, zero)

    for copy in copies[1:]:
        copy.wait()
    weights[...] = counts[...].astype(F32)
    cosine, sine = selection(recip[...], 1)
    basis_coef = jnp.sum(cosine * coef[...], axis=1, keepdims=True)
    for slot in range(slots):
        tile = sums[pl.ds(slot * BASIS, BASIS), :]
        potential[pl.ds(slot, 1), :] = jnp.sum(tile * basis_coef, axis=0, keepdims=True)
        rounded = tile.astype(BF16)
        lanes = pl.ds(slot * walkers, walkers)
        basis[:, lanes] = rounded
        for copy in range(3):
            basis_three[pl.ds(copy * BASIS, BASIS), lanes] = rounded

    cosine, sine = selection(recip[...], 3)
    select = jnp.concatenate([cosine, sine], axis=1)
    select_out[...] = select.T.astype(BF16)
    select = select.astype(BF16)
    part = lax.broadcasted_iota(jnp.int32, (3 * BASIS, w_two.shape[2]), 0) // BASIS
    heads = []
    for s in range(states):
        value = lax.dot_general(select, w_one_raw[:, s, :], NN, preferred_element_type=F32)
        high, middle, low = (p.astype(F32) for p in three_parts(value))
        value = jnp.where(part == 0, high, jnp.where(part == 1, middle, low))
        w_eff[s] = value.T.astype(BF16)
        value = w_two_raw[:, s, :]
        w_two[s] = value
        w_two_t[s] = value.astype(F32).T.astype(BF16)
        value = w_heads_raw[:, s, :].astype(F32)
        value = jnp.concatenate([value, jnp.zeros((16 - value.shape[0], value.shape[1]), F32)], axis=0)
        heads.append(value.astype(BF16))
        w_heads_t[s] = value.T.astype(BF16)

    for s in range(states):
        pre = lax.dot_general(w_eff[s], basis_three[...], NN, preferred_element_type=F32)
        first_act = jnp.tanh(pre)
        first[s] = first_act
        pre = lax.dot_general(w_two_t[s], first_act.astype(BF16), NN, preferred_element_type=F32)
        second_tanh = jnp.tanh(pre)
        second[s] = second_tanh
        second_bf = (second_tanh + first_act).astype(BF16)
        out = lax.dot_general(heads[s], second_bf, NN, preferred_element_type=F32)
        for slot in range(slots):
            at = slice(slot * walkers, (slot + 1) * walkers)
            send[pl.ds(s * 2 * slots + slot, 1), :] = jnp.tanh(out[0:1, at])
            send[pl.ds((s * 2 + 1) * slots + slot, 1), :] = out[1:2, at]


def invert_transposed(spread, gathered, slots, walkers):
    column = lax.broadcasted_iota(jnp.int32, (slots, walkers), 0)
    rows = []
    for j in range(slots):
        squashed = gathered[pl.ds(j, slots, stride=2 * slots), :]
        rows.append(jnp.where(column == j, 1.0, 0.0) + spread * squashed)
    for p in range(slots):
        factor = 1.0 / rows[p][p : p + 1, :]
        pivot = jnp.where(column == p, factor, rows[p] * factor)
        for r in range(slots):
            if r != p:
                rows[r] = jnp.where(column == p, 0.0, rows[r]) - rows[r][p : p + 1, :] * pivot
        rows[p] = pivot
    return rows


def energy_kernel(spread, *refs):
    near, (others, potential, weights_in, message, sums, d_amp, d_hps, gathered, inverse_t) = refs[:XS], refs[XS:]
    slots, walkers = potential.shape
    states = d_amp.shape[0]
    block = near[0].shape[0]
    me_x, me_core = lax.axis_index("x"), lax.axis_index("core")
    for k in range(XS):
        for at, source in ((me_core, near[k]), (1 - me_core, others.at[k])):
            owner = (me_x + XS - k) % XS * 2 + at
            gathered[pl.ds(pl.multiple_of(owner * block, block), block), :] = source[...]

    weights = weights_in[...]
    rows = invert_transposed(spread, gathered, slots, walkers)
    for j in range(slots):
        inverse_t[j] = rows[j]
    pot = potential[...]
    column = lax.broadcasted_iota(jnp.int32, (slots, walkers), 0)
    energies = [jnp.zeros((slots, walkers), F32) for _ in range(slots)]
    for j in range(slots):
        squashed = gathered[pl.ds(2 * slots * j, slots), :]
        amplitude = jnp.where(column == j, 1.0, 0.0) + spread * squashed
        hps = gathered[pl.ds(2 * slots * j + slots, slots), :] + pot * amplitude
        for k in range(slots):
            energies[k] = energies[k] + rows[j] * hps[k : k + 1, :]
    trace = jnp.zeros((1, walkers), F32)
    lane = lax.broadcasted_iota(jnp.int32, (8, walkers), 1)
    note = jnp.zeros((8, walkers), F32)
    for k in range(slots):
        trace = trace + energies[k][k : k + 1, :]
        total = jnp.sum(energies[k] * weights, axis=1, keepdims=True)
        for half in range(slots // 8):
            note = jnp.where(lane == half * slots + k, total[half * 8 : half * 8 + 8], note)
    count = jnp.sum(weights, axis=1, keepdims=True)
    level = jnp.sum(trace * weights, axis=1, keepdims=True)
    sums[...] = note
    lane = lane[0:1]
    note = jnp.where(lane == 0, level, jnp.where(lane == 1, count, 0.0))
    for d in range(message.shape[0]):
        message[d] = note
    for s in range(states):
        own = inverse_t[(me_x * 2 + me_core) * states + s]
        along_own = jnp.zeros((slots, walkers), F32)
        for k in range(slots):
            along_own = along_own + own[k : k + 1, :] * energies[k]
        d_amp[s] = weights * (2.0 * trace * own - along_own)
        d_hps[s] = weights * own


def backward_kernel(spread, *refs):
    (messages, d_amp, d_hps, sums, send, potential, basis, first, second, w_two, w_heads_t), outs, (
        out, cot, first_bf, inner_one, inner_two) = refs[:11], refs[11 : 11 + YS], refs[11 + YS :]
    states, slots, walkers = d_amp.shape
    hidden = w_two.shape[1]
    total = jnp.sum(messages[...], axis=0)
    share = 1.0 / total[:, 1:2]
    mean = total[:, 0:1] * share
    pot = potential[...]
    cot[...] = jnp.zeros(cot.shape, F32)
    for s in range(states):
        squashed = send[pl.ds(s * 2 * slots, slots), :]
        hps = d_hps[s] * share
        amp = (d_amp[s] - 2.0 * mean * d_hps[s]) * share
        amp = (amp + hps * pot) * (spread * (1.0 - squashed * squashed))
        for slot in range(slots):
            lanes = pl.ds(slot * walkers, walkers)
            cot[s, 0:1, lanes] = amp[slot : slot + 1, :]
            cot[s, 1:2, lanes] = hps[slot : slot + 1, :]

    def put(start, s, array):
        for half in range(hidden // 128):
            at = pl.ds(4 * start + 2 * half + s, array.shape[0], stride=4)
            out[at, :] = array[:, half * 128 : (half + 1) * 128]

    spare = 4 * (2 * COSINES - 1)
    out[pl.ds(spare, 4 * BASIS - spare), :] = jnp.zeros((4 * BASIS - spare, 128), F32)
    for s in range(states):
        first_act = first[s]
        second_tanh = second[s]
        second_bf = (second_tanh + first_act).astype(BF16)
        first_bf[s] = first_act.astype(BF16)
        cot_bf = cot[s].astype(BF16)
        heads = lax.dot_general(cot_bf, second_bf, NT, preferred_element_type=F32)
        put(2 * COSINES - 1, s, heads[0:2])
        back_two = lax.dot_general(w_heads_t[s], cot_bf, NN, preferred_element_type=F32)
        inner = (back_two * (1.0 - second_tanh * second_tanh)).astype(BF16)
        inner_two[s] = inner
        back_one = back_two + lax.dot_general(w_two[s], inner, NN, preferred_element_type=F32)
        inner_one[s] = (back_one * (1.0 - first_act * first_act)).astype(BF16)
    for s in range(states):
        put(BASIS, s, lax.dot_general(first_bf[s], inner_two[s], NT, preferred_element_type=F32))
        grad_one = lax.dot_general(basis[...], inner_one[s], NT, preferred_element_type=F32)
        put(0, s, grad_one[0 : 2 * COSINES - 1])
    out[pl.ds(4 * (2 * COSINES + 1), 8), :] = sums[...] * share
    part = out.shape[0] // YS
    y = lax.axis_index("y")
    for k in range(YS):
        outs[k][...] = out[pl.ds(pl.multiple_of((y + k) % YS * part, part), part), :]


def line_kernel(*refs):
    parts, out = refs[:YS], refs[YS]
    total = parts[0][...]
    for k in range(1, YS):
        total = total + parts[k][...]
    out[...] = total


def piece_kernel(parts, out):
    piece = parts[0]
    for z in range(1, ZS):
        piece = piece + parts[z]
    for z in range(ZS):
        out[z] = piece


def expand_kernel(*refs):
    parts, (select, energy, grad_first, grad_second, grad_heads, summed) = refs[:YS], refs[YS:]
    y = lax.axis_index("y")
    part = parts[0].shape[0]
    for k in range(YS):
        summed[pl.ds(pl.multiple_of((y + YS - k) % YS * part, part), part), :] = parts[k][...]
    slots = energy.shape[0]
    note = summed[pl.ds(4 * (2 * COSINES + 1), 8), :]
    for half in range(slots // 8):
        energy[pl.ds(half * 8, 8), :] = note[:, half * slots : (half + 1) * slots]
    for at in range(4):
        value = summed[pl.ds(at, BASIS, stride=4), :]
        parts = jnp.concatenate(three_parts(value), axis=0)
        rows = lax.dot_general(select[...], parts, NN, preferred_element_type=F32)
        grad_first[pl.ds(at, rows.shape[0], stride=4), :] = rows
    grad_second[...] = summed[pl.ds(4 * BASIS, grad_second.shape[0]), :]
    grad_heads[...] = summed[pl.ds(4 * (2 * COSINES - 1), grad_heads.shape[0]), :]


def call(body, outs, scratch, limit, args, flops, hbm=False):
    place = pltpu.HBM if hbm else pltpu.VMEM
    if hbm:
        args = [pltpu.with_memory_space_constraint(a, pltpu.HBM) for a in args]
    return pl.pallas_call(
        body,
        out_shape=[jax.ShapeDtypeStruct(s, t) for s, t in outs],
        in_specs=[pl.BlockSpec(memory_space=place)] * len(args),
        out_specs=[pl.BlockSpec(memory_space=pltpu.VMEM)] * len(outs),
        scratch_shapes=[pltpu.VMEM(*s) if isinstance(s, tuple) else s for s in scratch],
        compiler_params=pltpu.CompilerParams(vmem_limit_bytes=limit << 20),
        cost_estimate=pl.CostEstimate(flops=flops, bytes_accessed=1 << 20, transcendentals=0),
    )(*args)


def along(axis, array, shift):
    size = lax.axis_size(axis)
    return lax.ppermute(array, axis, [(d, (d + shift) % size) for d in range(size)])


def shards(positions, recip, moire_coef, counts, w_first, w_second, w_heads):
    electrons, slots, walkers = positions.shape[1:]
    features, states, hidden = w_first.shape
    rows = slots * walkers
    groups, shares = lax.axis_size(("x", "core")), lax.axis_size(("y", "z"))
    spread = 0.75 / slots
    total = 4 * (BASIS + hidden)
    work = 2 * states * rows * hidden * hidden
    args = (positions, recip, moire_coef[None], counts[None], w_first, w_second, w_heads)
    send, potential, basis, first, second, weights, select, w_two, w_heads_t = call(
        forward_kernel,
        [((4 * slots, walkers), F32), ((slots, walkers), F32), ((BASIS, rows), BF16),
         ((states, hidden, rows), F32), ((states, hidden, rows), F32), ((1, walkers), F32),
         ((features, 3 * BASIS), BF16), ((states, hidden, hidden), BF16), ((states, hidden, 16), BF16)],
        [(a.shape, a.dtype) for a in args] + [pltpu.SemaphoreType.DMA((len(args),))]
        + [((4, electrons, slots, walkers), F32), ((slots * BASIS, walkers), F32),
           ((states, hidden, 3 * BASIS), BF16), ((states, hidden, hidden), BF16), ((3 * BASIS, rows), BF16)],
        40, args, 2 * work, hbm=True)
    near = [send] + [along("x", send, k) for k in range(1, XS)]
    others = along("core", jnp.stack(near), 1)

    def energy_body(*refs):
        energy_kernel(spread, *refs)

    def backward_body(*refs):
        backward_kernel(spread, *refs)

    message, sums, d_amp, d_hps = call(
        energy_body,
        [((shares, 1, walkers), F32), ((8, walkers), F32), ((states, slots, walkers), F32),
         ((states, slots, walkers), F32)],
        [((groups * 4 * slots, walkers), F32), ((slots, slots, walkers), F32)],
        4, (*near, others, potential, weights), 1 << 20)
    messages = lax.all_to_all(message, ("y", "z"), 0, 0, tiled=True)
    part = total // YS
    size = part // ZS
    parts = call(
        backward_body,
        [((part, 128), F32)] * YS,
        [((total, 128), F32), ((states, 16, rows), F32), ((states, hidden, rows), BF16),
         ((states, hidden, rows), BF16), ((states, hidden, rows), BF16)],
        20, (messages, d_amp, d_hps, sums, send, potential, basis, first, second, w_two, w_heads_t), 3 * work)
    parts = [parts[0]] + [along("y", parts[k], k) for k in range(1, YS)]
    line, = call(line_kernel, [((part, 128), F32)], [], 4, parts, 1 << 20)
    lines = lax.all_to_all(line.reshape(ZS, size, 128), "z", 0, 0, tiled=True)
    pieces, = call(piece_kernel, [((ZS, size, 128), F32)], [], 4, (lines,), 1 << 20)
    summed = lax.all_to_all(pieces, "z", 0, 0, tiled=True).reshape(part, 128)
    parts = [summed] + [along("y", summed, k) for k in range(1, YS)]
    energy_matrix, *grads = call(
        expand_kernel,
        [((slots, slots), F32)] + [((4 * w.shape[0], 128), F32) for w in (w_first, w_second, w_heads)],
        [((total, 128), F32)], 8, (*parts, select), 1 << 20)
    grads = [g.reshape(-1, hidden // 128, states, 128).transpose(0, 2, 1, 3).reshape(-1, states, hidden) for g in grads]
    return (energy_matrix, *grads)


def solution(mesh):
    mesh = Mesh(mesh.devices.reshape(XS, 2, YS, ZS), ("x", "core", "y", "z"))
    state, walker = ("x", "core"), ("y", "z")
    in_specs = (
        P(None, None, None, walker),
        P(),
        P(),
        P(walker),
        P(None, state, None),
        P(None, state, None),
        P(None, state, None),
    )
    out_specs = (P(), P(None, state, None), P(None, state, None), P(None, state, None))
    return jax.shard_map(shards, mesh=mesh, in_specs=in_specs, out_specs=out_specs, check_vma=False)
```

```python
import jax
import jax.numpy as jnp
import numpy as np
from jax import lax
from jax.experimental import pallas as pl
from jax.experimental.pallas import tpu as pltpu
from jax.sharding import Mesh
from jax.sharding import PartitionSpec as P

F32 = jnp.float32
BF16 = jnp.bfloat16
INV_ROOT_THREE = 1.0 / 1.7320508075688772
XS, YS, ZS = 4, 4, 8
BASIS = 64
COSINES = 25
NN = (((1,), (0,)), ((), ()))
NT = (((1,), (1,)), ((), ()))


def half_turn_polynomials():
    squares = np.linspace(0.0, 0.25, 4001)
    root = np.sqrt(squares)
    ratio = np.where(root > 0, np.sin(np.pi * root) / np.where(root > 0, root, 1.0), np.pi)
    cheb = np.polynomial.chebyshev.Chebyshev
    sine = cheb.fit(squares, ratio, 5).convert(kind=np.polynomial.Polynomial).coef
    cosine = cheb.fit(squares, np.cos(np.pi * root), 6).convert(kind=np.polynomial.Polynomial).coef
    return [float(c) for c in sine], [float(c) for c in cosine]


SIN_COEF, COS_COEF = half_turn_polynomials()


def horner(coef, at):
    total = jnp.full_like(at, coef[-1])
    for c in coef[-2::-1]:
        total = total * at + c
    return total


def turn(t):
    rest = t - jnp.round(t)
    square = rest * rest
    sine = rest * horner(SIN_COEF, square)
    cosine = horner(COS_COEF, square)
    return 1.0 - 2.0 * sine * sine, 2.0 * sine * cosine


def mul(a, b):
    return a[0] * b[0] - a[1] * b[1], a[0] * b[1] + a[1] * b[0]


def selection(recip, copies):
    count = recip.shape[1]
    key = 7 * recip[0:1, :] + recip[1:2, :]
    size = jnp.abs(key)
    row = lax.broadcasted_iota(jnp.int32, (BASIS * copies, count), 0) % BASIS
    cosine = jnp.where(row == size, 1.0, 0.0)
    sign = jnp.where(key < 0, -1.0, 1.0)
    sine = jnp.where((row == size + (COSINES - 1)) & (size > 0), sign, 0.0)
    return cosine, sine


def three_parts(value):
    high = value.astype(BF16)
    rest = value - high.astype(F32)
    middle = rest.astype(BF16)
    low = (rest - middle.astype(F32)).astype(BF16)
    return high, middle, low


def forward_kernel(pos_in, recip_in, coef_in, counts_in, w_one_in, w_two_in, w_heads_in,
                   send, potential, basis, first, second, weights, select_out, w_two, w_heads_t,
                   pos, recip, coef, counts, w_one_raw, w_two_raw, w_heads_raw, arrived,
                   turns, sums, w_eff, w_two_t, basis_three):
    electrons, slots, walkers = pos.shape[1:]
    states = w_two.shape[0]
    copies = []
    for source, target in ((pos_in, pos), (recip_in, recip), (coef_in, coef), (counts_in, counts),
                           (w_one_in, w_one_raw), (w_two_in, w_two_raw), (w_heads_in, w_heads_raw)):
        copies.append(pltpu.make_async_copy(source, target, arrived.at[len(copies)]))
        copies[-1].start()
    copies[0].wait()

    def phases(e, carry):
        x, y = pos[0, e], pos[1, e]
        third = y * INV_ROOT_THREE
        turns[0, e], turns[1, e] = turn(x - third)
        turns[2, e], turns[3, e] = turn(2.0 * third)
        return carry

    lax.fori_loop(0, electrons, phases, 0, unroll=5)

    def powers(e, rows, at, upto):
        one = (turns[at, e, rows], turns[at + 1, e, rows])
        result = [one]
        for _ in range(upto - 1):
            result.append(mul(result[-1], one))
        return result

    for half in range(slots // 8):
        rows = pl.ds(half * 8, 8)

        def put(index, value, half=half):
            sums[pl.ds(half * 8 * BASIS + index, 8, stride=BASIS), :] = value

        zero = jnp.zeros((8, walkers), F32)
        for firsts in ((1, 2), (3,)):
            alone = 3 in firsts

            def add(e, totals, firsts=firsts, alone=alone, rows=rows):
                u, v = powers(e, rows, 0, 3 if alone else 2), powers(e, rows, 2, 3)
                parts = []
                for m in firsts:
                    for n in (1, 2, 3):
                        (cu, su), (cv, sv) = u[m - 1], v[n - 1]
                        parts += [cu * cv, su * sv, su * cv, cu * sv]
                if alone:
                    for p in u + v:
                        parts += list(p)
                return tuple(t + p for t, p in zip(totals, parts, strict=True))

            number = 12 * len(firsts) + (12 if alone else 0)
            totals = lax.fori_loop(0, electrons, add, (zero,) * number, unroll=6)
            for i, m in enumerate(firsts):
                for n in (1, 2, 3):
                    cc, ss, sc, cs = totals[12 * i + 4 * (n - 1) : 12 * i + 4 * n]
                    put(7 * m + n, cc - ss)
                    put(7 * m - n, cc + ss)
                    put(COSINES - 1 + 7 * m + n, sc + cs)
                    put(COSINES - 1 + 7 * m - n, sc - cs)
            if alone:
                rest = totals[12:]
                for m in (1, 2, 3):
                    put(7 * m, rest[2 * (m - 1)])
                    put(COSINES - 1 + 7 * m, rest[2 * (m - 1) + 1])
                    put(m, rest[6 + 2 * (m - 1)])
                    put(COSINES - 1 + m, rest[6 + 2 * (m - 1) + 1])
        put(0, jnp.full((8, walkers), float(electrons), F32))
        for index in range(2 * COSINES - 1, BASIS):
            put(index, zero)

    for copy in copies[1:]:
        copy.wait()
    weights[...] = counts[...].astype(F32)
    cosine, sine = selection(recip[...], 1)
    basis_coef = jnp.sum(cosine * coef[...], axis=1, keepdims=True)
    for slot in range(slots):
        tile = sums[pl.ds(slot * BASIS, BASIS), :]
        potential[pl.ds(slot, 1), :] = jnp.sum(tile * basis_coef, axis=0, keepdims=True)
        rounded = tile.astype(BF16)
        lanes = pl.ds(slot * walkers, walkers)
        basis[:, lanes] = rounded
        for copy in range(3):
            basis_three[pl.ds(copy * BASIS, BASIS), lanes] = rounded

    cosine, sine = selection(recip[...], 3)
    select = jnp.concatenate([cosine, sine], axis=1)
    select_out[...] = select.T.astype(BF16)
    select = select.astype(BF16)
    part = lax.broadcasted_iota(jnp.int32, (3 * BASIS, w_two.shape[2]), 0) // BASIS
    heads = []
    for s in range(states):
        value = lax.dot_general(select, w_one_raw[:, s, :], NN, preferred_element_type=F32)
        high, middle, low = (p.astype(F32) for p in three_parts(value))
        value = jnp.where(part == 0, high, jnp.where(part == 1, middle, low))
        w_eff[s] = value.T.astype(BF16)
        value = w_two_raw[:, s, :]
        w_two[s] = value
        w_two_t[s] = value.astype(F32).T.astype(BF16)
        value = w_heads_raw[:, s, :].astype(F32)
        value = jnp.concatenate([value, jnp.zeros((16 - value.shape[0], value.shape[1]), F32)], axis=0)
        heads.append(value.astype(BF16))
        w_heads_t[s] = value.T.astype(BF16)

    for s in range(states):
        pre = lax.dot_general(w_eff[s], basis_three[...], NN, preferred_element_type=F32)
        first_act = jnp.tanh(pre)
        first[s] = first_act
        pre = lax.dot_general(w_two_t[s], first_act.astype(BF16), NN, preferred_element_type=F32)
        second_tanh = jnp.tanh(pre)
        second[s] = second_tanh
        second_bf = (second_tanh + first_act).astype(BF16)
        out = lax.dot_general(heads[s], second_bf, NN, preferred_element_type=F32)
        for slot in range(slots):
            at = slice(slot * walkers, (slot + 1) * walkers)
            send[pl.ds(s * 2 * slots + slot, 1), :] = jnp.tanh(out[0:1, at])
            send[pl.ds((s * 2 + 1) * slots + slot, 1), :] = out[1:2, at]


def invert_transposed(spread, gathered, slots, walkers):
    column = lax.broadcasted_iota(jnp.int32, (slots, walkers), 0)
    rows = []
    for j in range(slots):
        squashed = gathered[pl.ds(j, slots, stride=2 * slots), :]
        rows.append(jnp.where(column == j, 1.0, 0.0) + spread * squashed)
    for p in range(slots):
        factor = 1.0 / rows[p][p : p + 1, :]
        pivot = jnp.where(column == p, factor, rows[p] * factor)
        for r in range(slots):
            if r != p:
                rows[r] = jnp.where(column == p, 0.0, rows[r]) - rows[r][p : p + 1, :] * pivot
        rows[p] = pivot
    return rows


def energy_kernel(spread, *refs):
    near, (others, potential, weights_in, message, sums, d_amp, d_hps, gathered, inverse_t) = refs[:XS], refs[XS:]
    slots, walkers = potential.shape
    states = d_amp.shape[0]
    block = near[0].shape[0]
    me_x, me_core = lax.axis_index("x"), lax.axis_index("core")
    for k in range(XS):
        for at, source in ((me_core, near[k]), (1 - me_core, others.at[k])):
            owner = (me_x + XS - k) % XS * 2 + at
            gathered[pl.ds(pl.multiple_of(owner * block, block), block), :] = source[...]

    weights = weights_in[...]
    rows = invert_transposed(spread, gathered, slots, walkers)
    for j in range(slots):
        inverse_t[j] = rows[j]
    pot = potential[...]
    column = lax.broadcasted_iota(jnp.int32, (slots, walkers), 0)
    energies = [jnp.zeros((slots, walkers), F32) for _ in range(slots)]
    for j in range(slots):
        squashed = gathered[pl.ds(2 * slots * j, slots), :]
        amplitude = jnp.where(column == j, 1.0, 0.0) + spread * squashed
        hps = gathered[pl.ds(2 * slots * j + slots, slots), :] + pot * amplitude
        for k in range(slots):
            energies[k] = energies[k] + rows[j] * hps[k : k + 1, :]
    trace = jnp.zeros((1, walkers), F32)
    lane = lax.broadcasted_iota(jnp.int32, (8, walkers), 1)
    note = jnp.zeros((8, walkers), F32)
    for k in range(slots):
        trace = trace + energies[k][k : k + 1, :]
        total = jnp.sum(energies[k] * weights, axis=1, keepdims=True)
        for half in range(slots // 8):
            note = jnp.where(lane == half * slots + k, total[half * 8 : half * 8 + 8], note)
    count = jnp.sum(weights, axis=1, keepdims=True)
    level = jnp.sum(trace * weights, axis=1, keepdims=True)
    sums[...] = note
    lane = lane[0:1]
    note = jnp.where(lane == 0, level, jnp.where(lane == 1, count, 0.0))
    for d in range(message.shape[0]):
        message[d] = note
    for s in range(states):
        own = inverse_t[(me_x * 2 + me_core) * states + s]
        along_own = jnp.zeros((slots, walkers), F32)
        for k in range(slots):
            along_own = along_own + own[k : k + 1, :] * energies[k]
        d_amp[s] = weights * (2.0 * trace * own - along_own)
        d_hps[s] = weights * own


def backward_kernel(spread, *refs):
    (messages, d_amp, d_hps, sums, send, potential, basis, first, second, w_two, w_heads_t), outs, (
        out, cot, first_bf, inner_one, inner_two) = refs[:11], refs[11 : 11 + YS], refs[11 + YS :]
    states, slots, walkers = d_amp.shape
    hidden = w_two.shape[1]
    total = jnp.sum(messages[...], axis=0)
    share = 1.0 / total[:, 1:2]
    mean = total[:, 0:1] * share
    pot = potential[...]
    cot[...] = jnp.zeros(cot.shape, F32)
    for s in range(states):
        squashed = send[pl.ds(s * 2 * slots, slots), :]
        hps = d_hps[s] * share
        amp = (d_amp[s] - 2.0 * mean * d_hps[s]) * share
        amp = (amp + hps * pot) * (spread * (1.0 - squashed * squashed))
        for slot in range(slots):
            lanes = pl.ds(slot * walkers, walkers)
            cot[s, 0:1, lanes] = amp[slot : slot + 1, :]
            cot[s, 1:2, lanes] = hps[slot : slot + 1, :]

    def put(start, s, array):
        for half in range(hidden // 128):
            at = pl.ds(4 * start + 2 * half + s, array.shape[0], stride=4)
            out[at, :] = array[:, half * 128 : (half + 1) * 128]

    spare = 4 * (2 * COSINES - 1)
    out[pl.ds(spare, 4 * BASIS - spare), :] = jnp.zeros((4 * BASIS - spare, 128), F32)
    for s in range(states):
        first_act = first[s]
        second_tanh = second[s]
        second_bf = (second_tanh + first_act).astype(BF16)
        first_bf[s] = first_act.astype(BF16)
        cot_bf = cot[s].astype(BF16)
        heads = lax.dot_general(cot_bf, second_bf, NT, preferred_element_type=F32)
        put(2 * COSINES - 1, s, heads[0:2])
        back_two = lax.dot_general(w_heads_t[s], cot_bf, NN, preferred_element_type=F32)
        inner = (back_two * (1.0 - second_tanh * second_tanh)).astype(BF16)
        inner_two[s] = inner
        back_one = back_two + lax.dot_general(w_two[s], inner, NN, preferred_element_type=F32)
        inner_one[s] = (back_one * (1.0 - first_act * first_act)).astype(BF16)
        grad_one = lax.dot_general(basis[...], inner_one[s], NT, preferred_element_type=F32)
        put(0, s, grad_one[0 : 2 * COSINES - 1])
        put(BASIS, s, lax.dot_general(first_bf[s], inner_two[s], NT, preferred_element_type=F32))
    out[pl.ds(4 * (2 * COSINES + 1), 8), :] = sums[...] * share
    part = out.shape[0] // YS
    y = lax.axis_index("y")
    for k in range(YS):
        outs[k][...] = out[pl.ds(pl.multiple_of((y + k) % YS * part, part), part), :]


def line_kernel(*refs):
    parts, out = refs[:YS], refs[YS]
    total = parts[0][...]
    for k in range(1, YS):
        total = total + parts[k][...]
    out[...] = total


def piece_kernel(parts, out):
    piece = parts[0]
    for z in range(1, ZS):
        piece = piece + parts[z]
    for z in range(ZS):
        out[z] = piece


def expand_kernel(*refs):
    parts, (select, energy, grad_first, grad_second, grad_heads, summed) = refs[:YS], refs[YS:]
    y = lax.axis_index("y")
    part = parts[0].shape[0]
    for k in range(YS):
        summed[pl.ds(pl.multiple_of((y + YS - k) % YS * part, part), part), :] = parts[k][...]
    slots = energy.shape[0]
    note = summed[pl.ds(4 * (2 * COSINES + 1), 8), :]
    for half in range(slots // 8):
        energy[pl.ds(half * 8, 8), :] = note[:, half * slots : (half + 1) * slots]
    for at in range(4):
        value = summed[pl.ds(at, BASIS, stride=4), :]
        parts = jnp.concatenate(three_parts(value), axis=0)
        rows = lax.dot_general(select[...], parts, NN, preferred_element_type=F32)
        grad_first[pl.ds(at, rows.shape[0], stride=4), :] = rows
    grad_second[...] = summed[pl.ds(4 * BASIS, grad_second.shape[0]), :]
    grad_heads[...] = summed[pl.ds(4 * (2 * COSINES - 1), grad_heads.shape[0]), :]


def call(body, outs, scratch, limit, args, flops, hbm=False):
    place = pltpu.HBM if hbm else pltpu.VMEM
    if hbm:
        args = [pltpu.with_memory_space_constraint(a, pltpu.HBM) for a in args]
    return pl.pallas_call(
        body,
        out_shape=[jax.ShapeDtypeStruct(s, t) for s, t in outs],
        in_specs=[pl.BlockSpec(memory_space=place)] * len(args),
        out_specs=[pl.BlockSpec(memory_space=pltpu.VMEM)] * len(outs),
        scratch_shapes=[pltpu.VMEM(*s) if isinstance(s, tuple) else s for s in scratch],
        compiler_params=pltpu.CompilerParams(vmem_limit_bytes=limit << 20),
        cost_estimate=pl.CostEstimate(flops=flops, bytes_accessed=1 << 20, transcendentals=0),
    )(*args)


def along(axis, array, shift):
    size = lax.axis_size(axis)
    return lax.ppermute(array, axis, [(d, (d + shift) % size) for d in range(size)])


def shards(positions, recip, moire_coef, counts, w_first, w_second, w_heads):
    electrons, slots, walkers = positions.shape[1:]
    features, states, hidden = w_first.shape
    rows = slots * walkers
    groups, shares = lax.axis_size(("x", "core")), lax.axis_size(("y", "z"))
    spread = 0.75 / slots
    total = 4 * (BASIS + hidden)
    work = 2 * states * rows * hidden * hidden
    args = (positions, recip, moire_coef[None], counts[None], w_first, w_second, w_heads)
    send, potential, basis, first, second, weights, select, w_two, w_heads_t = call(
        forward_kernel,
        [((4 * slots, walkers), F32), ((slots, walkers), F32), ((BASIS, rows), BF16),
         ((states, hidden, rows), F32), ((states, hidden, rows), F32), ((1, walkers), F32),
         ((features, 3 * BASIS), BF16), ((states, hidden, hidden), BF16), ((states, hidden, 16), BF16)],
        [(a.shape, a.dtype) for a in args] + [pltpu.SemaphoreType.DMA((len(args),))]
        + [((4, electrons, slots, walkers), F32), ((slots * BASIS, walkers), F32),
           ((states, hidden, 3 * BASIS), BF16), ((states, hidden, hidden), BF16), ((3 * BASIS, rows), BF16)],
        40, args, 2 * work, hbm=True)
    near = [send] + [along("x", send, k) for k in range(1, XS)]
    others = along("core", jnp.stack(near), 1)

    def energy_body(*refs):
        energy_kernel(spread, *refs)

    def backward_body(*refs):
        backward_kernel(spread, *refs)

    message, sums, d_amp, d_hps = call(
        energy_body,
        [((shares, 1, walkers), F32), ((8, walkers), F32), ((states, slots, walkers), F32),
         ((states, slots, walkers), F32)],
        [((groups * 4 * slots, walkers), F32), ((slots, slots, walkers), F32)],
        4, (*near, others, potential, weights), 1 << 20)
    messages = lax.all_to_all(message, ("y", "z"), 0, 0, tiled=True)
    part = total // YS
    size = part // ZS
    parts = call(
        backward_body,
        [((part, 128), F32)] * YS,
        [((total, 128), F32), ((states, 16, rows), F32), ((states, hidden, rows), BF16),
         ((states, hidden, rows), BF16), ((states, hidden, rows), BF16)],
        20, (messages, d_amp, d_hps, sums, send, potential, basis, first, second, w_two, w_heads_t), 3 * work)
    parts = [parts[0]] + [along("y", parts[k], k) for k in range(1, YS)]
    line, = call(line_kernel, [((part, 128), F32)], [], 4, parts, 1 << 20)
    lines = lax.all_to_all(line.reshape(ZS, size, 128), "z", 0, 0, tiled=True)
    pieces, = call(piece_kernel, [((ZS, size, 128), F32)], [], 4, (lines,), 1 << 20)
    summed = lax.all_to_all(pieces, "z", 0, 0, tiled=True).reshape(part, 128)
    parts = [summed] + [along("y", summed, k) for k in range(1, YS)]
    energy_matrix, *grads = call(
        expand_kernel,
        [((slots, slots), F32)] + [((4 * w.shape[0], 128), F32) for w in (w_first, w_second, w_heads)],
        [((total, 128), F32)], 8, (*parts, select), 1 << 20)
    grads = [g.reshape(-1, hidden // 128, states, 128).transpose(0, 2, 1, 3).reshape(-1, states, hidden) for g in grads]
    return (energy_matrix, *grads)


def solution(mesh):
    mesh = Mesh(mesh.devices.reshape(XS, 2, YS, ZS), ("x", "core", "y", "z"))
    state, walker = ("x", "core"), ("y", "z")
    in_specs = (
        P(None, None, None, walker),
        P(),
        P(),
        P(walker),
        P(None, state, None),
        P(None, state, None),
        P(None, state, None),
    )
    out_specs = (P(), P(None, state, None), P(None, state, None), P(None, state, None))
    return jax.shard_map(shards, mesh=mesh, in_specs=in_specs, out_specs=out_specs, check_vma=False)
```

```python
import jax
import jax.numpy as jnp
import numpy as np
from jax import lax
from jax.experimental import pallas as pl
from jax.experimental.pallas import tpu as pltpu
from jax.sharding import Mesh
from jax.sharding import PartitionSpec as P

F32 = jnp.float32
BF16 = jnp.bfloat16
INV_ROOT_THREE = 1.0 / 1.7320508075688772
XS, YS, ZS = 4, 4, 8
BASIS = 64
COSINES = 25
NN = (((1,), (0,)), ((), ()))
NT = (((1,), (1,)), ((), ()))


def half_turn_polynomials():
    squares = np.linspace(0.0, 0.25, 4001)
    root = np.sqrt(squares)
    ratio = np.where(root > 0, np.sin(np.pi * root) / np.where(root > 0, root, 1.0), np.pi)
    cheb = np.polynomial.chebyshev.Chebyshev
    sine = cheb.fit(squares, ratio, 5).convert(kind=np.polynomial.Polynomial).coef
    cosine = cheb.fit(squares, np.cos(np.pi * root), 6).convert(kind=np.polynomial.Polynomial).coef
    return [float(c) for c in sine], [float(c) for c in cosine]


SIN_COEF, COS_COEF = half_turn_polynomials()


def horner(coef, at):
    total = jnp.full_like(at, coef[-1])
    for c in coef[-2::-1]:
        total = total * at + c
    return total


def turn(t):
    rest = t - jnp.round(t)
    square = rest * rest
    sine = rest * horner(SIN_COEF, square)
    cosine = horner(COS_COEF, square)
    return 1.0 - 2.0 * sine * sine, 2.0 * sine * cosine


def mul(a, b):
    return a[0] * b[0] - a[1] * b[1], a[0] * b[1] + a[1] * b[0]


def selection(recip, copies):
    count = recip.shape[1]
    key = 7 * recip[0:1, :] + recip[1:2, :]
    size = jnp.abs(key)
    row = lax.broadcasted_iota(jnp.int32, (BASIS * copies, count), 0) % BASIS
    cosine = jnp.where(row == size, 1.0, 0.0)
    sign = jnp.where(key < 0, -1.0, 1.0)
    sine = jnp.where((row == size + (COSINES - 1)) & (size > 0), sign, 0.0)
    return cosine, sine


def three_parts(value):
    high = value.astype(BF16)
    rest = value - high.astype(F32)
    middle = rest.astype(BF16)
    low = (rest - middle.astype(F32)).astype(BF16)
    return high, middle, low


def forward_kernel(pos_in, recip_in, coef_in, counts_in, w_one_in, w_two_in, w_heads_in,
                   send, potential, basis, first, second, weights, select_out, w_two, w_heads_t,
                   pos, recip, coef, counts, w_one_raw, w_two_raw, w_heads_raw, arrived,
                   turns, sums, w_eff, w_two_t, basis_three):
    electrons, slots, walkers = pos.shape[1:]
    states = w_two.shape[0]
    copies = []
    for source, target in ((pos_in, pos), (recip_in, recip), (coef_in, coef), (counts_in, counts),
                           (w_one_in, w_one_raw), (w_two_in, w_two_raw), (w_heads_in, w_heads_raw)):
        copies.append(pltpu.make_async_copy(source, target, arrived.at[len(copies)]))
        copies[-1].start()
    copies[0].wait()

    def phases(e, carry):
        x, y = pos[0, e], pos[1, e]
        third = y * INV_ROOT_THREE
        turns[0, e], turns[1, e] = turn(x - third)
        turns[2, e], turns[3, e] = turn(2.0 * third)
        return carry

    lax.fori_loop(0, electrons, phases, 0, unroll=5)

    def powers(e, rows, at, upto):
        one = (turns[at, e, rows], turns[at + 1, e, rows])
        result = [one]
        for _ in range(upto - 1):
            result.append(mul(result[-1], one))
        return result

    for half in range(slots // 8):
        rows = pl.ds(half * 8, 8)

        def put(index, value, half=half):
            sums[pl.ds(half * 8 * BASIS + index, 8, stride=BASIS), :] = value

        zero = jnp.zeros((8, walkers), F32)
        for firsts in ((1, 2), (3,)):
            alone = 3 in firsts

            def add(e, totals, firsts=firsts, alone=alone, rows=rows):
                u, v = powers(e, rows, 0, 3 if alone else 2), powers(e, rows, 2, 3)
                parts = []
                for m in firsts:
                    for n in (1, 2, 3):
                        (cu, su), (cv, sv) = u[m - 1], v[n - 1]
                        parts += [cu * cv, su * sv, su * cv, cu * sv]
                if alone:
                    for p in u + v:
                        parts += list(p)
                return tuple(t + p for t, p in zip(totals, parts, strict=True))

            number = 12 * len(firsts) + (12 if alone else 0)
            totals = lax.fori_loop(0, electrons, add, (zero,) * number, unroll=6)
            for i, m in enumerate(firsts):
                for n in (1, 2, 3):
                    cc, ss, sc, cs = totals[12 * i + 4 * (n - 1) : 12 * i + 4 * n]
                    put(7 * m + n, cc - ss)
                    put(7 * m - n, cc + ss)
                    put(COSINES - 1 + 7 * m + n, sc + cs)
                    put(COSINES - 1 + 7 * m - n, sc - cs)
            if alone:
                rest = totals[12:]
                for m in (1, 2, 3):
                    put(7 * m, rest[2 * (m - 1)])
                    put(COSINES - 1 + 7 * m, rest[2 * (m - 1) + 1])
                    put(m, rest[6 + 2 * (m - 1)])
                    put(COSINES - 1 + m, rest[6 + 2 * (m - 1) + 1])
        put(0, jnp.full((8, walkers), float(electrons), F32))
        for index in range(2 * COSINES - 1, BASIS):
            put(index, zero)

    for copy in copies[1:]:
        copy.wait()
    weights[...] = counts[...].astype(F32)
    cosine, sine = selection(recip[...], 1)
    basis_coef = jnp.sum(cosine * coef[...], axis=1, keepdims=True)
    for slot in range(slots):
        tile = sums[pl.ds(slot * BASIS, BASIS), :]
        potential[pl.ds(slot, 1), :] = jnp.sum(tile * basis_coef, axis=0, keepdims=True)
        rounded = tile.astype(BF16)
        lanes = pl.ds(slot * walkers, walkers)
        basis[:, lanes] = rounded
        for copy in range(3):
            basis_three[pl.ds(copy * BASIS, BASIS), lanes] = rounded

    cosine, sine = selection(recip[...], 3)
    select = jnp.concatenate([cosine, sine], axis=1)
    select_out[...] = select.T.astype(BF16)
    select = select.astype(BF16)
    part = lax.broadcasted_iota(jnp.int32, (3 * BASIS, w_two.shape[2]), 0) // BASIS
    heads = []
    for s in range(states):
        value = lax.dot_general(select, w_one_raw[:, s, :], NN, preferred_element_type=F32)
        high, middle, low = (p.astype(F32) for p in three_parts(value))
        value = jnp.where(part == 0, high, jnp.where(part == 1, middle, low))
        w_eff[s] = value.T.astype(BF16)
        value = w_two_raw[:, s, :]
        w_two[s] = value
        w_two_t[s] = value.astype(F32).T.astype(BF16)
        value = w_heads_raw[:, s, :].astype(F32)
        value = jnp.concatenate([value, jnp.zeros((16 - value.shape[0], value.shape[1]), F32)], axis=0)
        heads.append(value.astype(BF16))
        w_heads_t[s] = value.T.astype(BF16)

    for s in range(states):
        pre = lax.dot_general(w_eff[s], basis_three[...], NN, preferred_element_type=F32)
        first_act = jnp.tanh(pre)
        first[s] = first_act
        pre = lax.dot_general(w_two_t[s], first_act.astype(BF16), NN, preferred_element_type=F32)
        second_tanh = jnp.tanh(pre)
        second[s] = second_tanh
        second_bf = (second_tanh + first_act).astype(BF16)
        out = lax.dot_general(heads[s], second_bf, NN, preferred_element_type=F32)
        for slot in range(slots):
            at = slice(slot * walkers, (slot + 1) * walkers)
            send[pl.ds(s * 2 * slots + slot, 1), :] = jnp.tanh(out[0:1, at])
            send[pl.ds((s * 2 + 1) * slots + slot, 1), :] = out[1:2, at]


def invert_transposed(spread, gathered, slots, walkers):
    column = lax.broadcasted_iota(jnp.int32, (slots, walkers), 0)
    rows = []
    for j in range(slots):
        squashed = gathered[pl.ds(j, slots, stride=2 * slots), :]
        rows.append(jnp.where(column == j, 1.0, 0.0) + spread * squashed)
    for p in range(slots):
        factor = 1.0 / rows[p][p : p + 1, :]
        pivot = jnp.where(column == p, factor, rows[p] * factor)
        for r in range(slots):
            if r != p:
                rows[r] = jnp.where(column == p, 0.0, rows[r]) - rows[r][p : p + 1, :] * pivot
        rows[p] = pivot
    return rows


def energy_kernel(spread, *refs):
    near, others = refs[:XS], refs[XS : 2 * XS]
    potential, weights_in, message, sums, d_amp, d_hps, gathered, inverse_t = refs[2 * XS :]
    slots, walkers = potential.shape
    states = d_amp.shape[0]
    block = near[0].shape[0]
    me_x, me_core = lax.axis_index("x"), lax.axis_index("core")
    for k in range(XS):
        for at, source in ((me_core, near[k]), (1 - me_core, others[k])):
            owner = (me_x + XS - k) % XS * 2 + at
            gathered[pl.ds(pl.multiple_of(owner * block, block), block), :] = source[...]

    weights = weights_in[...]
    rows = invert_transposed(spread, gathered, slots, walkers)
    for j in range(slots):
        inverse_t[j] = rows[j]
    pot = potential[...]
    column = lax.broadcasted_iota(jnp.int32, (slots, walkers), 0)
    energies = [jnp.zeros((slots, walkers), F32) for _ in range(slots)]
    for j in range(slots):
        squashed = gathered[pl.ds(2 * slots * j, slots), :]
        amplitude = jnp.where(column == j, 1.0, 0.0) + spread * squashed
        hps = gathered[pl.ds(2 * slots * j + slots, slots), :] + pot * amplitude
        for k in range(slots):
            energies[k] = energies[k] + rows[j] * hps[k : k + 1, :]
    trace = jnp.zeros((1, walkers), F32)
    lane = lax.broadcasted_iota(jnp.int32, (8, walkers), 1)
    note = jnp.zeros((8, walkers), F32)
    for k in range(slots):
        trace = trace + energies[k][k : k + 1, :]
        total = jnp.sum(energies[k] * weights, axis=1, keepdims=True)
        for half in range(slots // 8):
            note = jnp.where(lane == half * slots + k, total[half * 8 : half * 8 + 8], note)
    count = jnp.sum(weights, axis=1, keepdims=True)
    level = jnp.sum(trace * weights, axis=1, keepdims=True)
    sums[...] = note
    lane = lane[0:1]
    note = jnp.where(lane == 0, level, jnp.where(lane == 1, count, 0.0))
    for d in range(message.shape[0]):
        message[d] = note
    for s in range(states):
        own = inverse_t[(me_x * 2 + me_core) * states + s]
        along_own = jnp.zeros((slots, walkers), F32)
        for k in range(slots):
            along_own = along_own + own[k : k + 1, :] * energies[k]
        d_amp[s] = weights * (2.0 * trace * own - along_own)
        d_hps[s] = weights * own


def backward_kernel(spread, *refs):
    (messages, d_amp, d_hps, sums, send, potential, basis, first, second, w_two, w_heads_t), outs, (
        out, cot, first_bf, inner_one, inner_two) = refs[:11], refs[11 : 11 + YS], refs[11 + YS :]
    states, slots, walkers = d_amp.shape
    hidden = w_two.shape[1]
    total = jnp.sum(messages[...], axis=0)
    share = 1.0 / total[:, 1:2]
    mean = total[:, 0:1] * share
    pot = potential[...]
    cot[...] = jnp.zeros(cot.shape, F32)
    for s in range(states):
        squashed = send[pl.ds(s * 2 * slots, slots), :]
        hps = d_hps[s] * share
        amp = (d_amp[s] - 2.0 * mean * d_hps[s]) * share
        amp = (amp + hps * pot) * (spread * (1.0 - squashed * squashed))
        for slot in range(slots):
            lanes = pl.ds(slot * walkers, walkers)
            cot[s, 0:1, lanes] = amp[slot : slot + 1, :]
            cot[s, 1:2, lanes] = hps[slot : slot + 1, :]

    def put(start, s, array):
        for half in range(hidden // 128):
            at = pl.ds(4 * start + 2 * half + s, array.shape[0], stride=4)
            out[at, :] = array[:, half * 128 : (half + 1) * 128]

    spare = 4 * (2 * COSINES - 1)
    out[pl.ds(spare, 4 * BASIS - spare), :] = jnp.zeros((4 * BASIS - spare, 128), F32)
    for s in range(states):
        first_act = first[s]
        second_tanh = second[s]
        second_bf = (second_tanh + first_act).astype(BF16)
        first_bf[s] = first_act.astype(BF16)
        cot_bf = cot[s].astype(BF16)
        heads = lax.dot_general(cot_bf, second_bf, NT, preferred_element_type=F32)
        put(2 * COSINES - 1, s, heads[0:2])
        back_two = lax.dot_general(w_heads_t[s], cot_bf, NN, preferred_element_type=F32)
        inner = (back_two * (1.0 - second_tanh * second_tanh)).astype(BF16)
        inner_two[s] = inner
        back_one = back_two + lax.dot_general(w_two[s], inner, NN, preferred_element_type=F32)
        inner_one[s] = (back_one * (1.0 - first_act * first_act)).astype(BF16)
        grad_one = lax.dot_general(basis[...], inner_one[s], NT, preferred_element_type=F32)
        put(0, s, grad_one[0 : 2 * COSINES - 1])
        put(BASIS, s, lax.dot_general(first_bf[s], inner_two[s], NT, preferred_element_type=F32))
    out[pl.ds(4 * (2 * COSINES + 1), 8), :] = sums[...] * share
    part = out.shape[0] // YS
    y = lax.axis_index("y")
    for k in range(YS):
        outs[k][...] = out[pl.ds(pl.multiple_of((y + k) % YS * part, part), part), :]


def line_kernel(*refs):
    parts, out = refs[:YS], refs[YS]
    total = parts[0][...]
    for k in range(1, YS):
        total = total + parts[k][...]
    out[...] = total


def piece_kernel(parts, out):
    piece = parts[0]
    for z in range(1, ZS):
        piece = piece + parts[z]
    for z in range(ZS):
        out[z] = piece


def expand_kernel(*refs):
    parts, (select, energy, grad_first, grad_second, grad_heads, summed) = refs[:YS], refs[YS:]
    y = lax.axis_index("y")
    part = parts[0].shape[0]
    for k in range(YS):
        summed[pl.ds(pl.multiple_of((y + YS - k) % YS * part, part), part), :] = parts[k][...]
    slots = energy.shape[0]
    note = summed[pl.ds(4 * (2 * COSINES + 1), 8), :]
    for half in range(slots // 8):
        energy[pl.ds(half * 8, 8), :] = note[:, half * slots : (half + 1) * slots]
    for at in range(4):
        value = summed[pl.ds(at, BASIS, stride=4), :]
        parts = jnp.concatenate(three_parts(value), axis=0)
        rows = lax.dot_general(select[...], parts, NN, preferred_element_type=F32)
        grad_first[pl.ds(at, rows.shape[0], stride=4), :] = rows
    grad_second[...] = summed[pl.ds(4 * BASIS, grad_second.shape[0]), :]
    grad_heads[...] = summed[pl.ds(4 * (2 * COSINES - 1), grad_heads.shape[0]), :]


def call(body, outs, scratch, limit, args, flops, hbm=False):
    place = pltpu.HBM if hbm else pltpu.VMEM
    if hbm:
        args = [pltpu.with_memory_space_constraint(a, pltpu.HBM) for a in args]
    return pl.pallas_call(
        body,
        out_shape=[jax.ShapeDtypeStruct(s, t) for s, t in outs],
        in_specs=[pl.BlockSpec(memory_space=place)] * len(args),
        out_specs=[pl.BlockSpec(memory_space=pltpu.VMEM)] * len(outs),
        scratch_shapes=[pltpu.VMEM(*s) if isinstance(s, tuple) else s for s in scratch],
        compiler_params=pltpu.CompilerParams(vmem_limit_bytes=limit << 20),
        cost_estimate=pl.CostEstimate(flops=flops, bytes_accessed=1 << 20, transcendentals=0),
    )(*args)


def along(axis, array, shift):
    size = lax.axis_size(axis)
    return lax.ppermute(array, axis, [(d, (d + shift) % size) for d in range(size)])


def shards(positions, recip, moire_coef, counts, w_first, w_second, w_heads):
    electrons, slots, walkers = positions.shape[1:]
    features, states, hidden = w_first.shape
    rows = slots * walkers
    groups, shares = lax.axis_size(("x", "core")), lax.axis_size(("y", "z"))
    spread = 0.75 / slots
    total = 4 * (BASIS + hidden)
    work = 2 * states * rows * hidden * hidden
    args = (positions, recip, moire_coef[None], counts[None], w_first, w_second, w_heads)
    send, potential, basis, first, second, weights, select, w_two, w_heads_t = call(
        forward_kernel,
        [((4 * slots, walkers), F32), ((slots, walkers), F32), ((BASIS, rows), BF16),
         ((states, hidden, rows), F32), ((states, hidden, rows), F32), ((1, walkers), F32),
         ((features, 3 * BASIS), BF16), ((states, hidden, hidden), BF16), ((states, hidden, 16), BF16)],
        [(a.shape, a.dtype) for a in args] + [pltpu.SemaphoreType.DMA((len(args),))]
        + [((4, electrons, slots, walkers), F32), ((slots * BASIS, walkers), F32),
           ((states, hidden, 3 * BASIS), BF16), ((states, hidden, hidden), BF16), ((3 * BASIS, rows), BF16)],
        40, args, 2 * work, hbm=True)
    near = [send] + [along("x", send, k) for k in range(1, XS)]
    others = [along("core", block, 1) for block in near]

    def energy_body(*refs):
        energy_kernel(spread, *refs)

    def backward_body(*refs):
        backward_kernel(spread, *refs)

    message, sums, d_amp, d_hps = call(
        energy_body,
        [((shares, 1, walkers), F32), ((8, walkers), F32), ((states, slots, walkers), F32),
         ((states, slots, walkers), F32)],
        [((groups * 4 * slots, walkers), F32), ((slots, slots, walkers), F32)],
        4, (*near, *others, potential, weights), 1 << 20)
    messages = lax.all_to_all(message, ("y", "z"), 0, 0, tiled=True)
    part = total // YS
    size = part // ZS
    parts = call(
        backward_body,
        [((part, 128), F32)] * YS,
        [((total, 128), F32), ((states, 16, rows), F32), ((states, hidden, rows), BF16),
         ((states, hidden, rows), BF16), ((states, hidden, rows), BF16)],
        20, (messages, d_amp, d_hps, sums, send, potential, basis, first, second, w_two, w_heads_t), 3 * work)
    parts = [parts[0]] + [along("y", parts[k], k) for k in range(1, YS)]
    line, = call(line_kernel, [((part, 128), F32)], [], 4, parts, 1 << 20)
    lines = lax.all_to_all(line.reshape(ZS, size, 128), "z", 0, 0, tiled=True)
    pieces, = call(piece_kernel, [((ZS, size, 128), F32)], [], 4, (lines,), 1 << 20)
    summed = lax.all_to_all(pieces, "z", 0, 0, tiled=True).reshape(part, 128)
    parts = [summed] + [along("y", summed, k) for k in range(1, YS)]
    energy_matrix, *grads = call(
        expand_kernel,
        [((slots, slots), F32)] + [((4 * w.shape[0], 128), F32) for w in (w_first, w_second, w_heads)],
        [((total, 128), F32)], 8, (*parts, select), 1 << 20)
    grads = [g.reshape(-1, hidden // 128, states, 128).transpose(0, 2, 1, 3).reshape(-1, states, hidden) for g in grads]
    return (energy_matrix, *grads)


def solution(mesh):
    mesh = Mesh(mesh.devices.reshape(XS, 2, YS, ZS), ("x", "core", "y", "z"))
    state, walker = ("x", "core"), ("y", "z")
    in_specs = (
        P(None, None, None, walker),
        P(),
        P(),
        P(walker),
        P(None, state, None),
        P(None, state, None),
        P(None, state, None),
    )
    out_specs = (P(), P(None, state, None), P(None, state, None), P(None, state, None))
    return jax.shard_map(shards, mesh=mesh, in_specs=in_specs, out_specs=out_specs, check_vma=False)
```

```python
import jax
import jax.numpy as jnp
import numpy as np
from jax import lax
from jax.experimental import pallas as pl
from jax.experimental.pallas import tpu as pltpu
from jax.sharding import Mesh
from jax.sharding import PartitionSpec as P

F32 = jnp.float32
BF16 = jnp.bfloat16
INV_ROOT_THREE = 1.0 / 1.7320508075688772
XS, YS, ZS = 4, 4, 8
BASIS = 64
COSINES = 25
NN = (((1,), (0,)), ((), ()))
NT = (((1,), (1,)), ((), ()))


def half_turn_polynomials():
    squares = np.linspace(0.0, 0.25, 4001)
    root = np.sqrt(squares)
    ratio = np.where(root > 0, np.sin(np.pi * root) / np.where(root > 0, root, 1.0), np.pi)
    cheb = np.polynomial.chebyshev.Chebyshev
    sine = cheb.fit(squares, ratio, 5).convert(kind=np.polynomial.Polynomial).coef
    cosine = cheb.fit(squares, np.cos(np.pi * root), 6).convert(kind=np.polynomial.Polynomial).coef
    return [float(c) for c in sine], [float(c) for c in cosine]


SIN_COEF, COS_COEF = half_turn_polynomials()


def horner(coef, at):
    total = jnp.full_like(at, coef[-1])
    for c in coef[-2::-1]:
        total = total * at + c
    return total


def turn(t):
    rest = t - jnp.round(t)
    square = rest * rest
    sine = rest * horner(SIN_COEF, square)
    cosine = horner(COS_COEF, square)
    return 1.0 - 2.0 * sine * sine, 2.0 * sine * cosine


def mul(a, b):
    return a[0] * b[0] - a[1] * b[1], a[0] * b[1] + a[1] * b[0]


def selection(recip, copies):
    count = recip.shape[1]
    key = 7 * recip[0:1, :] + recip[1:2, :]
    size = jnp.abs(key)
    row = lax.broadcasted_iota(jnp.int32, (BASIS * copies, count), 0) % BASIS
    cosine = jnp.where(row == size, 1.0, 0.0)
    sign = jnp.where(key < 0, -1.0, 1.0)
    sine = jnp.where((row == size + (COSINES - 1)) & (size > 0), sign, 0.0)
    return cosine, sine


def three_parts(value):
    high = value.astype(BF16)
    rest = value - high.astype(F32)
    middle = rest.astype(BF16)
    low = (rest - middle.astype(F32)).astype(BF16)
    return high, middle, low


def forward_kernel(pos_in, recip_in, coef_in, counts_in, w_one_in, w_two_in, w_heads_in,
                   send, potential, basis, first, second, weights, select_out, w_two, w_heads_t,
                   pos, recip, coef, counts, w_one_raw, w_two_raw, w_heads_raw, arrived,
                   turns, sums, w_eff, w_two_t, basis_three):
    electrons, slots, walkers = pos.shape[1:]
    states = w_two.shape[0]
    copies = []
    for source, target in ((pos_in, pos), (recip_in, recip), (coef_in, coef), (counts_in, counts),
                           (w_one_in, w_one_raw), (w_two_in, w_two_raw), (w_heads_in, w_heads_raw)):
        copies.append(pltpu.make_async_copy(source, target, arrived.at[len(copies)]))
        copies[-1].start()
    copies[0].wait()

    def phases(e, carry):
        x, y = pos[0, e], pos[1, e]
        third = y * INV_ROOT_THREE
        turns[0, e], turns[1, e] = turn(x - third)
        turns[2, e], turns[3, e] = turn(2.0 * third)
        return carry

    lax.fori_loop(0, electrons, phases, 0, unroll=10)

    def powers(e, rows, at, upto):
        one = (turns[at, e, rows], turns[at + 1, e, rows])
        result = [one]
        for _ in range(upto - 1):
            result.append(mul(result[-1], one))
        return result

    for half in range(slots // 8):
        rows = pl.ds(half * 8, 8)

        def put(index, value, half=half):
            sums[pl.ds(half * 8 * BASIS + index, 8, stride=BASIS), :] = value

        zero = jnp.zeros((8, walkers), F32)
        for firsts in ((1, 2), (3,)):
            alone = 3 in firsts

            def add(e, totals, firsts=firsts, alone=alone, rows=rows):
                u, v = powers(e, rows, 0, 3 if alone else 2), powers(e, rows, 2, 3)
                parts = []
                for m in firsts:
                    for n in (1, 2, 3):
                        (cu, su), (cv, sv) = u[m - 1], v[n - 1]
                        parts += [cu * cv, su * sv, su * cv, cu * sv]
                if alone:
                    for p in u + v:
                        parts += list(p)
                return tuple(t + p for t, p in zip(totals, parts, strict=True))

            number = 12 * len(firsts) + (12 if alone else 0)
            totals = lax.fori_loop(0, electrons, add, (zero,) * number, unroll=10)
            for i, m in enumerate(firsts):
                for n in (1, 2, 3):
                    cc, ss, sc, cs = totals[12 * i + 4 * (n - 1) : 12 * i + 4 * n]
                    put(7 * m + n, cc - ss)
                    put(7 * m - n, cc + ss)
                    put(COSINES - 1 + 7 * m + n, sc + cs)
                    put(COSINES - 1 + 7 * m - n, sc - cs)
            if alone:
                rest = totals[12:]
                for m in (1, 2, 3):
                    put(7 * m, rest[2 * (m - 1)])
                    put(COSINES - 1 + 7 * m, rest[2 * (m - 1) + 1])
                    put(m, rest[6 + 2 * (m - 1)])
                    put(COSINES - 1 + m, rest[6 + 2 * (m - 1) + 1])
        put(0, jnp.full((8, walkers), float(electrons), F32))
        for index in range(2 * COSINES - 1, BASIS):
            put(index, zero)

    for copy in copies[1:]:
        copy.wait()
    weights[...] = counts[...].astype(F32)
    cosine, sine = selection(recip[...], 1)
    basis_coef = jnp.sum(cosine * coef[...], axis=1, keepdims=True)
    for slot in range(slots):
        tile = sums[pl.ds(slot * BASIS, BASIS), :]
        potential[pl.ds(slot, 1), :] = jnp.sum(tile * basis_coef, axis=0, keepdims=True)
        rounded = tile.astype(BF16)
        lanes = pl.ds(slot * walkers, walkers)
        basis[:, lanes] = rounded
        for copy in range(3):
            basis_three[pl.ds(copy * BASIS, BASIS), lanes] = rounded

    cosine, sine = selection(recip[...], 3)
    select = jnp.concatenate([cosine, sine], axis=1)
    select_out[...] = select.T.astype(BF16)
    select = select.astype(BF16)
    part = lax.broadcasted_iota(jnp.int32, (3 * BASIS, w_two.shape[2]), 0) // BASIS
    heads = []
    for s in range(states):
        value = lax.dot_general(select, w_one_raw[:, s, :], NN, preferred_element_type=F32)
        high, middle, low = (p.astype(F32) for p in three_parts(value))
        value = jnp.where(part == 0, high, jnp.where(part == 1, middle, low))
        w_eff[s] = value.T.astype(BF16)
        value = w_two_raw[:, s, :]
        w_two[s] = value
        w_two_t[s] = value.astype(F32).T.astype(BF16)
        value = w_heads_raw[:, s, :].astype(F32)
        value = jnp.concatenate([value, jnp.zeros((16 - value.shape[0], value.shape[1]), F32)], axis=0)
        heads.append(value.astype(BF16))
        w_heads_t[s] = value.T.astype(BF16)

    for s in range(states):
        pre = lax.dot_general(w_eff[s], basis_three[...], NN, preferred_element_type=F32)
        first_act = jnp.tanh(pre)
        first[s] = first_act
        pre = lax.dot_general(w_two_t[s], first_act.astype(BF16), NN, preferred_element_type=F32)
        second_tanh = jnp.tanh(pre)
        second[s] = second_tanh
        second_bf = (second_tanh + first_act).astype(BF16)
        out = lax.dot_general(heads[s], second_bf, NN, preferred_element_type=F32)
        for slot in range(slots):
            at = slice(slot * walkers, (slot + 1) * walkers)
            send[pl.ds(s * 2 * slots + slot, 1), :] = jnp.tanh(out[0:1, at])
            send[pl.ds((s * 2 + 1) * slots + slot, 1), :] = out[1:2, at]


def invert_transposed(spread, gathered, slots, walkers):
    column = lax.broadcasted_iota(jnp.int32, (slots, walkers), 0)
    rows = []
    for j in range(slots):
        squashed = gathered[pl.ds(j, slots, stride=2 * slots), :]
        rows.append(jnp.where(column == j, 1.0, 0.0) + spread * squashed)
    for p in range(slots):
        factor = 1.0 / rows[p][p : p + 1, :]
        pivot = jnp.where(column == p, factor, rows[p] * factor)
        for r in range(slots):
            if r != p:
                rows[r] = jnp.where(column == p, 0.0, rows[r]) - rows[r][p : p + 1, :] * pivot
        rows[p] = pivot
    return rows


def energy_kernel(spread, *refs):
    near, others = refs[:XS], refs[XS : 2 * XS]
    potential, weights_in, message, sums, d_amp, d_hps, gathered, inverse_t = refs[2 * XS :]
    slots, walkers = potential.shape
    states = d_amp.shape[0]
    block = near[0].shape[0]
    me_x, me_core = lax.axis_index("x"), lax.axis_index("core")
    for k in range(XS):
        for at, source in ((me_core, near[k]), (1 - me_core, others[k])):
            owner = (me_x + XS - k) % XS * 2 + at
            gathered[pl.ds(pl.multiple_of(owner * block, block), block), :] = source[...]

    weights = weights_in[...]
    rows = invert_transposed(spread, gathered, slots, walkers)
    for j in range(slots):
        inverse_t[j] = rows[j]
    pot = potential[...]
    column = lax.broadcasted_iota(jnp.int32, (slots, walkers), 0)
    energies = [jnp.zeros((slots, walkers), F32) for _ in range(slots)]
    for j in range(slots):
        squashed = gathered[pl.ds(2 * slots * j, slots), :]
        amplitude = jnp.where(column == j, 1.0, 0.0) + spread * squashed
        hps = gathered[pl.ds(2 * slots * j + slots, slots), :] + pot * amplitude
        for k in range(slots):
            energies[k] = energies[k] + rows[j] * hps[k : k + 1, :]
    trace = jnp.zeros((1, walkers), F32)
    lane = lax.broadcasted_iota(jnp.int32, (8, walkers), 1)
    note = jnp.zeros((8, walkers), F32)
    for k in range(slots):
        trace = trace + energies[k][k : k + 1, :]
        total = jnp.sum(energies[k] * weights, axis=1, keepdims=True)
        for half in range(slots // 8):
            note = jnp.where(lane == half * slots + k, total[half * 8 : half * 8 + 8], note)
    count = jnp.sum(weights, axis=1, keepdims=True)
    level = jnp.sum(trace * weights, axis=1, keepdims=True)
    sums[...] = note
    lane = lane[0:1]
    note = jnp.where(lane == 0, level, jnp.where(lane == 1, count, 0.0))
    for d in range(message.shape[0]):
        message[d] = note
    for s in range(states):
        own = inverse_t[(me_x * 2 + me_core) * states + s]
        along_own = jnp.zeros((slots, walkers), F32)
        for k in range(slots):
            along_own = along_own + own[k : k + 1, :] * energies[k]
        d_amp[s] = weights * (2.0 * trace * own - along_own)
        d_hps[s] = weights * own


def backward_kernel(spread, *refs):
    (messages, d_amp, d_hps, sums, send, potential, basis, first, second, w_two, w_heads_t), outs, (
        out, cot, first_bf, inner_one, inner_two) = refs[:11], refs[11 : 11 + YS], refs[11 + YS :]
    states, slots, walkers = d_amp.shape
    hidden = w_two.shape[1]
    total = jnp.sum(messages[...], axis=0)
    share = 1.0 / total[:, 1:2]
    mean = total[:, 0:1] * share
    pot = potential[...]
    cot[...] = jnp.zeros(cot.shape, F32)
    for s in range(states):
        squashed = send[pl.ds(s * 2 * slots, slots), :]
        hps = d_hps[s] * share
        amp = (d_amp[s] - 2.0 * mean * d_hps[s]) * share
        amp = (amp + hps * pot) * (spread * (1.0 - squashed * squashed))
        for slot in range(slots):
            lanes = pl.ds(slot * walkers, walkers)
            cot[s, 0:1, lanes] = amp[slot : slot + 1, :]
            cot[s, 1:2, lanes] = hps[slot : slot + 1, :]

    def put(start, s, array):
        for half in range(hidden // 128):
            at = pl.ds(4 * start + 2 * half + s, array.shape[0], stride=4)
            out[at, :] = array[:, half * 128 : (half + 1) * 128]

    spare = 4 * (2 * COSINES - 1)
    out[pl.ds(spare, 4 * BASIS - spare), :] = jnp.zeros((4 * BASIS - spare, 128), F32)
    for s in range(states):
        first_act = first[s]
        second_tanh = second[s]
        second_bf = (second_tanh + first_act).astype(BF16)
        first_bf[s] = first_act.astype(BF16)
        cot_bf = cot[s].astype(BF16)
        heads = lax.dot_general(cot_bf, second_bf, NT, preferred_element_type=F32)
        put(2 * COSINES - 1, s, heads[0:2])
        back_two = lax.dot_general(w_heads_t[s], cot_bf, NN, preferred_element_type=F32)
        inner = (back_two * (1.0 - second_tanh * second_tanh)).astype(BF16)
        inner_two[s] = inner
        back_one = back_two + lax.dot_general(w_two[s], inner, NN, preferred_element_type=F32)
        inner_one[s] = (back_one * (1.0 - first_act * first_act)).astype(BF16)
        grad_one = lax.dot_general(basis[...], inner_one[s], NT, preferred_element_type=F32)
        put(0, s, grad_one[0 : 2 * COSINES - 1])
        put(BASIS, s, lax.dot_general(first_bf[s], inner_two[s], NT, preferred_element_type=F32))
    out[pl.ds(4 * (2 * COSINES + 1), 8), :] = sums[...] * share
    part = out.shape[0] // YS
    y = lax.axis_index("y")
    for k in range(YS):
        outs[k][...] = out[pl.ds(pl.multiple_of((y + k) % YS * part, part), part), :]


def line_kernel(*refs):
    parts, out = refs[:YS], refs[YS]
    total = parts[0][...]
    for k in range(1, YS):
        total = total + parts[k][...]
    out[...] = total


def piece_kernel(parts, out):
    piece = parts[0]
    for z in range(1, ZS):
        piece = piece + parts[z]
    for z in range(ZS):
        out[z] = piece


def expand_kernel(*refs):
    parts, (select, energy, grad_first, grad_second, grad_heads, summed) = refs[:YS], refs[YS:]
    y = lax.axis_index("y")
    part = parts[0].shape[0]
    for k in range(YS):
        summed[pl.ds(pl.multiple_of((y + YS - k) % YS * part, part), part), :] = parts[k][...]
    slots = energy.shape[0]
    note = summed[pl.ds(4 * (2 * COSINES + 1), 8), :]
    for half in range(slots // 8):
        energy[pl.ds(half * 8, 8), :] = note[:, half * slots : (half + 1) * slots]
    value = jnp.concatenate([summed[pl.ds(at, BASIS, stride=4), :] for at in range(4)], axis=1)
    rows = lax.dot_general(select[...], jnp.concatenate(three_parts(value), axis=0), NN, preferred_element_type=F32)
    for at in range(4):
        grad_first[pl.ds(at, rows.shape[0], stride=4), :] = rows[:, at * 128 : (at + 1) * 128]
    grad_second[...] = summed[pl.ds(4 * BASIS, grad_second.shape[0]), :]
    grad_heads[...] = summed[pl.ds(4 * (2 * COSINES - 1), grad_heads.shape[0]), :]


def call(body, outs, scratch, limit, args, flops, hbm=False):
    place = pltpu.HBM if hbm else pltpu.VMEM
    if hbm:
        args = [pltpu.with_memory_space_constraint(a, pltpu.HBM) for a in args]
    return pl.pallas_call(
        body,
        out_shape=[jax.ShapeDtypeStruct(s, t) for s, t in outs],
        in_specs=[pl.BlockSpec(memory_space=place)] * len(args),
        out_specs=[pl.BlockSpec(memory_space=pltpu.VMEM)] * len(outs),
        scratch_shapes=[pltpu.VMEM(*s) if isinstance(s, tuple) else s for s in scratch],
        compiler_params=pltpu.CompilerParams(vmem_limit_bytes=limit << 20),
        cost_estimate=pl.CostEstimate(flops=flops, bytes_accessed=1 << 20, transcendentals=0),
    )(*args)


def along(axis, array, shift):
    size = lax.axis_size(axis)
    return lax.ppermute(array, axis, [(d, (d + shift) % size) for d in range(size)])


def shards(positions, recip, moire_coef, counts, w_first, w_second, w_heads):
    electrons, slots, walkers = positions.shape[1:]
    features, states, hidden = w_first.shape
    rows = slots * walkers
    groups, shares = lax.axis_size(("x", "core")), lax.axis_size(("y", "z"))
    spread = 0.75 / slots
    total = 4 * (BASIS + hidden)
    work = 2 * states * rows * hidden * hidden
    args = (positions, recip, moire_coef[None], counts[None], w_first, w_second, w_heads)
    send, potential, basis, first, second, weights, select, w_two, w_heads_t = call(
        forward_kernel,
        [((4 * slots, walkers), F32), ((slots, walkers), F32), ((BASIS, rows), BF16),
         ((states, hidden, rows), F32), ((states, hidden, rows), F32), ((1, walkers), F32),
         ((features, 3 * BASIS), BF16), ((states, hidden, hidden), BF16), ((states, hidden, 16), BF16)],
        [(a.shape, a.dtype) for a in args] + [pltpu.SemaphoreType.DMA((len(args),))]
        + [((4, electrons, slots, walkers), F32), ((slots * BASIS, walkers), F32),
           ((states, hidden, 3 * BASIS), BF16), ((states, hidden, hidden), BF16), ((3 * BASIS, rows), BF16)],
        40, args, 2 * work, hbm=True)
    near = [send] + [along("x", send, k) for k in range(1, XS)]
    others = [along("core", block, 1) for block in near]

    def energy_body(*refs):
        energy_kernel(spread, *refs)

    def backward_body(*refs):
        backward_kernel(spread, *refs)

    message, sums, d_amp, d_hps = call(
        energy_body,
        [((shares, 1, walkers), F32), ((8, walkers), F32), ((states, slots, walkers), F32),
         ((states, slots, walkers), F32)],
        [((groups * 4 * slots, walkers), F32), ((slots, slots, walkers), F32)],
        4, (*near, *others, potential, weights), 1 << 20)
    messages = lax.all_to_all(message, ("y", "z"), 0, 0, tiled=True)
    part = total // YS
    size = part // ZS
    parts = call(
        backward_body,
        [((part, 128), F32)] * YS,
        [((total, 128), F32), ((states, 16, rows), F32), ((states, hidden, rows), BF16),
         ((states, hidden, rows), BF16), ((states, hidden, rows), BF16)],
        20, (messages, d_amp, d_hps, sums, send, potential, basis, first, second, w_two, w_heads_t), 3 * work)
    parts = [parts[0]] + [along("y", parts[k], k) for k in range(1, YS)]
    line, = call(line_kernel, [((part, 128), F32)], [], 4, parts, 1 << 20)
    lines = lax.all_to_all(line.reshape(ZS, size, 128), "z", 0, 0, tiled=True)
    pieces, = call(piece_kernel, [((ZS, size, 128), F32)], [], 4, (lines,), 1 << 20)
    summed = lax.all_to_all(pieces, "z", 0, 0, tiled=True).reshape(part, 128)
    parts = [summed] + [along("y", summed, k) for k in range(1, YS)]
    energy_matrix, *grads = call(
        expand_kernel,
        [((slots, slots), F32)] + [((4 * w.shape[0], 128), F32) for w in (w_first, w_second, w_heads)],
        [((total, 128), F32)], 8, (*parts, select), 1 << 20)
    grads = [g.reshape(-1, hidden // 128, states, 128).transpose(0, 2, 1, 3).reshape(-1, states, hidden) for g in grads]
    return (energy_matrix, *grads)


def solution(mesh):
    mesh = Mesh(mesh.devices.reshape(XS, 2, YS, ZS), ("x", "core", "y", "z"))
    state, walker = ("x", "core"), ("y", "z")
    in_specs = (
        P(None, None, None, walker),
        P(),
        P(),
        P(walker),
        P(None, state, None),
        P(None, state, None),
        P(None, state, None),
    )
    out_specs = (P(), P(None, state, None), P(None, state, None), P(None, state, None))
    return jax.shard_map(shards, mesh=mesh, in_specs=in_specs, out_specs=out_specs, check_vma=False)
```

```python
import jax
import jax.numpy as jnp
import numpy as np
from jax import lax
from jax.experimental import pallas as pl
from jax.experimental.pallas import tpu as pltpu
from jax.sharding import Mesh
from jax.sharding import PartitionSpec as P

F32 = jnp.float32
BF16 = jnp.bfloat16
INV_ROOT_THREE = 1.0 / 1.7320508075688772
XS, YS, ZS = 4, 4, 8
BASIS = 64
COSINES = 25
NN = (((1,), (0,)), ((), ()))
NT = (((1,), (1,)), ((), ()))


def half_turn_polynomials():
    squares = np.linspace(0.0, 0.25, 4001)
    root = np.sqrt(squares)
    ratio = np.where(root > 0, np.sin(np.pi * root) / np.where(root > 0, root, 1.0), np.pi)
    cheb = np.polynomial.chebyshev.Chebyshev
    sine = cheb.fit(squares, ratio, 5).convert(kind=np.polynomial.Polynomial).coef
    cosine = cheb.fit(squares, np.cos(np.pi * root), 6).convert(kind=np.polynomial.Polynomial).coef
    return [float(c) for c in sine], [float(c) for c in cosine]


SIN_COEF, COS_COEF = half_turn_polynomials()


def horner(coef, at):
    total = jnp.full_like(at, coef[-1])
    for c in coef[-2::-1]:
        total = total * at + c
    return total


def turn(t):
    rest = t - jnp.round(t)
    square = rest * rest
    sine = rest * horner(SIN_COEF, square)
    cosine = horner(COS_COEF, square)
    return 1.0 - 2.0 * sine * sine, 2.0 * sine * cosine


def mul(a, b):
    return a[0] * b[0] - a[1] * b[1], a[0] * b[1] + a[1] * b[0]


def selection(recip, copies):
    count = recip.shape[1]
    key = 7 * recip[0:1, :] + recip[1:2, :]
    size = jnp.abs(key)
    row = lax.broadcasted_iota(jnp.int32, (BASIS * copies, count), 0) % BASIS
    cosine = jnp.where(row == size, 1.0, 0.0)
    sign = jnp.where(key < 0, -1.0, 1.0)
    sine = jnp.where((row == size + (COSINES - 1)) & (size > 0), sign, 0.0)
    return cosine, sine


def three_parts(value):
    high = value.astype(BF16)
    rest = value - high.astype(F32)
    middle = rest.astype(BF16)
    low = (rest - middle.astype(F32)).astype(BF16)
    return high, middle, low


def forward_kernel(pos_in, recip_in, coef_in, counts_in, w_one_in, w_two_in, w_heads_in,
                   send, potential, basis, first, second, weights, select_out, w_two, w_heads_t,
                   pos, recip, coef, counts, w_one_raw, w_two_raw, w_heads_raw, arrived,
                   turns, sums, w_eff, w_two_t, basis_three):
    electrons, slots, walkers = pos.shape[1:]
    states = w_two.shape[0]
    copies = []
    for source, target in ((pos_in, pos), (recip_in, recip), (coef_in, coef), (counts_in, counts),
                           (w_one_in, w_one_raw), (w_two_in, w_two_raw), (w_heads_in, w_heads_raw)):
        copies.append(pltpu.make_async_copy(source, target, arrived.at[len(copies)]))
        copies[-1].start()
    copies[0].wait()

    def phases(e, carry):
        x, y = pos[0, e], pos[1, e]
        third = y * INV_ROOT_THREE
        turns[0, e], turns[1, e] = turn(x - third)
        turns[2, e], turns[3, e] = turn(2.0 * third)
        return carry

    lax.fori_loop(0, electrons, phases, 0, unroll=10)

    def powers(e, rows, at, upto):
        one = (turns[at, e, rows], turns[at + 1, e, rows])
        result = [one]
        for _ in range(upto - 1):
            result.append(mul(result[-1], one))
        return result

    for half in range(slots // 8):
        rows = pl.ds(half * 8, 8)

        def put(index, value, half=half):
            sums[pl.ds(half * 8 * BASIS + index, 8, stride=BASIS), :] = value

        zero = jnp.zeros((8, walkers), F32)
        for firsts in ((1, 2), (3,)):
            alone = 3 in firsts

            def add(e, totals, firsts=firsts, alone=alone, rows=rows):
                u, v = powers(e, rows, 0, 3 if alone else 2), powers(e, rows, 2, 3)
                parts = []
                for m in firsts:
                    for n in (1, 2, 3):
                        (cu, su), (cv, sv) = u[m - 1], v[n - 1]
                        parts += [cu * cv, su * sv, su * cv, cu * sv]
                if alone:
                    for p in u + v:
                        parts += list(p)
                return tuple(t + p for t, p in zip(totals, parts, strict=True))

            number = 12 * len(firsts) + (12 if alone else 0)
            totals = lax.fori_loop(0, electrons, add, (zero,) * number, unroll=10)
            for i, m in enumerate(firsts):
                for n in (1, 2, 3):
                    cc, ss, sc, cs = totals[12 * i + 4 * (n - 1) : 12 * i + 4 * n]
                    put(7 * m + n, cc - ss)
                    put(7 * m - n, cc + ss)
                    put(COSINES - 1 + 7 * m + n, sc + cs)
                    put(COSINES - 1 + 7 * m - n, sc - cs)
            if alone:
                rest = totals[12:]
                for m in (1, 2, 3):
                    put(7 * m, rest[2 * (m - 1)])
                    put(COSINES - 1 + 7 * m, rest[2 * (m - 1) + 1])
                    put(m, rest[6 + 2 * (m - 1)])
                    put(COSINES - 1 + m, rest[6 + 2 * (m - 1) + 1])
        put(0, jnp.full((8, walkers), float(electrons), F32))
        for index in range(2 * COSINES - 1, BASIS):
            put(index, zero)

    for copy in copies[1:]:
        copy.wait()
    weights[...] = counts[...].astype(F32)
    cosine, sine = selection(recip[...], 1)
    basis_coef = jnp.sum(cosine * coef[...], axis=1, keepdims=True)
    for slot in range(slots):
        tile = sums[pl.ds(slot * BASIS, BASIS), :]
        potential[pl.ds(slot, 1), :] = jnp.sum(tile * basis_coef, axis=0, keepdims=True)
        rounded = tile.astype(BF16)
        lanes = pl.ds(slot * walkers, walkers)
        basis[:, lanes] = rounded
        for copy in range(3):
            basis_three[pl.ds(copy * BASIS, BASIS), lanes] = rounded

    cosine, sine = selection(recip[...], 3)
    select = jnp.concatenate([cosine, sine], axis=1)
    select_out[...] = select.T.astype(BF16)
    select = select.astype(BF16)
    part = lax.broadcasted_iota(jnp.int32, (3 * BASIS, w_two.shape[2]), 0) // BASIS
    heads = []
    for s in range(states):
        value = lax.dot_general(select, w_one_raw[:, s, :], NN, preferred_element_type=F32)
        high, middle, low = (p.astype(F32) for p in three_parts(value))
        value = jnp.where(part == 0, high, jnp.where(part == 1, middle, low))
        w_eff[s] = value.T.astype(BF16)
        value = w_two_raw[:, s, :]
        w_two[s] = value
        w_two_t[s] = value.astype(F32).T.astype(BF16)
        value = w_heads_raw[:, s, :].astype(F32)
        value = jnp.concatenate([value, jnp.zeros((16 - value.shape[0], value.shape[1]), F32)], axis=0)
        heads.append(value.astype(BF16))
        w_heads_t[s] = value.T.astype(BF16)

    for s in range(states):
        pre = lax.dot_general(w_eff[s], basis_three[...], NN, preferred_element_type=F32)
        first_act = jnp.tanh(pre)
        first[s] = first_act
        pre = lax.dot_general(w_two_t[s], first_act.astype(BF16), NN, preferred_element_type=F32)
        second_tanh = jnp.tanh(pre)
        second[s] = second_tanh
        second_bf = (second_tanh + first_act).astype(BF16)
        out = lax.dot_general(heads[s], second_bf, NN, preferred_element_type=F32)
        for slot in range(slots):
            at = slice(slot * walkers, (slot + 1) * walkers)
            send[pl.ds(s * 2 * slots + slot, 1), :] = jnp.tanh(out[0:1, at])
            send[pl.ds((s * 2 + 1) * slots + slot, 1), :] = out[1:2, at]


def invert_transposed(spread, gathered, slots, walkers):
    column = lax.broadcasted_iota(jnp.int32, (slots, walkers), 0)
    rows = []
    for j in range(slots):
        squashed = gathered[pl.ds(j, slots, stride=2 * slots), :]
        rows.append(jnp.where(column == j, 1.0, 0.0) + spread * squashed)
    for p in range(slots):
        factor = 1.0 / rows[p][p : p + 1, :]
        pivot = jnp.where(column == p, factor, rows[p] * factor)
        for r in range(slots):
            if r != p:
                rows[r] = jnp.where(column == p, 0.0, rows[r]) - rows[r][p : p + 1, :] * pivot
        rows[p] = pivot
    return rows


def energy_kernel(spread, *refs):
    near, others = refs[:XS], refs[XS : 2 * XS]
    potential, weights_in, message, sums, d_amp, d_hps, gathered, inverse_t = refs[2 * XS :]
    slots, walkers = potential.shape
    states = d_amp.shape[0]
    block = near[0].shape[0]
    me_x, me_core = lax.axis_index("x"), lax.axis_index("core")
    for k in range(XS):
        for at, source in ((me_core, near[k]), (1 - me_core, others[k])):
            owner = (me_x + XS - k) % XS * 2 + at
            gathered[pl.ds(pl.multiple_of(owner * block, block), block), :] = source[...]

    weights = weights_in[...]
    rows = invert_transposed(spread, gathered, slots, walkers)
    for j in range(slots):
        inverse_t[j] = rows[j]
    pot = potential[...]
    column = lax.broadcasted_iota(jnp.int32, (slots, walkers), 0)
    energies = [jnp.zeros((slots, walkers), F32) for _ in range(slots)]
    for j in range(slots):
        squashed = gathered[pl.ds(2 * slots * j, slots), :]
        amplitude = jnp.where(column == j, 1.0, 0.0) + spread * squashed
        hps = gathered[pl.ds(2 * slots * j + slots, slots), :] + pot * amplitude
        for k in range(slots):
            energies[k] = energies[k] + rows[j] * hps[k : k + 1, :]
    trace = jnp.zeros((1, walkers), F32)
    lane = lax.broadcasted_iota(jnp.int32, (8, walkers), 1)
    note = jnp.zeros((8, walkers), F32)
    for k in range(slots):
        trace = trace + energies[k][k : k + 1, :]
        total = jnp.sum(energies[k] * weights, axis=1, keepdims=True)
        for half in range(slots // 8):
            note = jnp.where(lane == half * slots + k, total[half * 8 : half * 8 + 8], note)
    count = jnp.sum(weights, axis=1, keepdims=True)
    level = jnp.sum(trace * weights, axis=1, keepdims=True)
    sums[...] = note
    lane = lane[0:1]
    note = jnp.where(lane == 0, level, jnp.where(lane == 1, count, 0.0))
    for d in range(message.shape[0]):
        message[d] = note
    for s in range(states):
        own = inverse_t[(me_x * 2 + me_core) * states + s]
        along_own = jnp.zeros((slots, walkers), F32)
        for k in range(slots):
            along_own = along_own + own[k : k + 1, :] * energies[k]
        d_amp[s] = weights * (2.0 * trace * own - along_own)
        d_hps[s] = weights * own


def backward_kernel(spread, *refs):
    (messages, d_amp, d_hps, sums, send, potential, basis, first, second, w_two, w_heads_t), outs, (
        out, cot) = refs[:11], refs[11 : 11 + YS], refs[11 + YS :]
    states, slots, walkers = d_amp.shape
    hidden = w_two.shape[1]
    total = jnp.sum(messages[...], axis=0)
    share = 1.0 / total[:, 1:2]
    mean = total[:, 0:1] * share
    pot = potential[...]
    cot[...] = jnp.zeros(cot.shape, F32)
    for s in range(states):
        squashed = send[pl.ds(s * 2 * slots, slots), :]
        hps = d_hps[s] * share
        amp = (d_amp[s] - 2.0 * mean * d_hps[s]) * share
        amp = (amp + hps * pot) * (spread * (1.0 - squashed * squashed))
        for slot in range(slots):
            lanes = pl.ds(slot * walkers, walkers)
            cot[s, 0:1, lanes] = amp[slot : slot + 1, :]
            cot[s, 1:2, lanes] = hps[slot : slot + 1, :]

    def put(start, s, array):
        for half in range(hidden // 128):
            at = pl.ds(4 * start + 2 * half + s, array.shape[0], stride=4)
            out[at, :] = array[:, half * 128 : (half + 1) * 128]

    spare = 4 * (2 * COSINES - 1)
    out[pl.ds(spare, 4 * BASIS - spare), :] = jnp.zeros((4 * BASIS - spare, 128), F32)
    for s in range(states):
        first_act = first[s]
        second_tanh = second[s]
        second_bf = (second_tanh + first_act).astype(BF16)
        first_bf = first_act.astype(BF16)
        cot_bf = cot[s].astype(BF16)
        heads = lax.dot_general(cot_bf, second_bf, NT, preferred_element_type=F32)
        put(2 * COSINES - 1, s, heads[0:2])
        back_two = lax.dot_general(w_heads_t[s], cot_bf, NN, preferred_element_type=F32)
        inner = (back_two * (1.0 - second_tanh * second_tanh)).astype(BF16)
        back_one = back_two + lax.dot_general(w_two[s], inner, NN, preferred_element_type=F32)
        inner_one = (back_one * (1.0 - first_act * first_act)).astype(BF16)
        grad_one = lax.dot_general(basis[...], inner_one, NT, preferred_element_type=F32)
        put(0, s, grad_one[0 : 2 * COSINES - 1])
        put(BASIS, s, lax.dot_general(first_bf, inner, NT, preferred_element_type=F32))
    out[pl.ds(4 * (2 * COSINES + 1), 8), :] = sums[...] * share
    part = out.shape[0] // YS
    y = lax.axis_index("y")
    for k in range(YS):
        outs[k][...] = out[pl.ds(pl.multiple_of((y + k) % YS * part, part), part), :]


def line_kernel(*refs):
    parts, out = refs[:YS], refs[YS]
    total = parts[0][...]
    for k in range(1, YS):
        total = total + parts[k][...]
    out[...] = total


def piece_kernel(parts, out):
    piece = parts[0]
    for z in range(1, ZS):
        piece = piece + parts[z]
    for z in range(ZS):
        out[z] = piece


def expand_kernel(*refs):
    parts, (select, energy, grad_first, grad_second, grad_heads, summed) = refs[:YS], refs[YS:]
    y = lax.axis_index("y")
    part = parts[0].shape[0]
    for k in range(YS):
        summed[pl.ds(pl.multiple_of((y + YS - k) % YS * part, part), part), :] = parts[k][...]
    slots = energy.shape[0]
    note = summed[pl.ds(4 * (2 * COSINES + 1), 8), :]
    for half in range(slots // 8):
        energy[pl.ds(half * 8, 8), :] = note[:, half * slots : (half + 1) * slots]
    value = jnp.concatenate([summed[pl.ds(at, BASIS, stride=4), :] for at in range(4)], axis=1)
    rows = lax.dot_general(select[...], jnp.concatenate(three_parts(value), axis=0), NN, preferred_element_type=F32)
    for at in range(4):
        grad_first[pl.ds(at, rows.shape[0], stride=4), :] = rows[:, at * 128 : (at + 1) * 128]
    grad_second[...] = summed[pl.ds(4 * BASIS, grad_second.shape[0]), :]
    grad_heads[...] = summed[pl.ds(4 * (2 * COSINES - 1), grad_heads.shape[0]), :]


def call(body, outs, scratch, limit, args, flops, hbm=False):
    place = pltpu.HBM if hbm else pltpu.VMEM
    if hbm:
        args = [pltpu.with_memory_space_constraint(a, pltpu.HBM) for a in args]
    return pl.pallas_call(
        body,
        out_shape=[jax.ShapeDtypeStruct(s, t) for s, t in outs],
        in_specs=[pl.BlockSpec(memory_space=place)] * len(args),
        out_specs=[pl.BlockSpec(memory_space=pltpu.VMEM)] * len(outs),
        scratch_shapes=[pltpu.VMEM(*s) if isinstance(s, tuple) else s for s in scratch],
        compiler_params=pltpu.CompilerParams(vmem_limit_bytes=limit << 20),
        cost_estimate=pl.CostEstimate(flops=flops, bytes_accessed=1 << 20, transcendentals=0),
    )(*args)


def along(axis, array, shift):
    size = lax.axis_size(axis)
    return lax.ppermute(array, axis, [(d, (d + shift) % size) for d in range(size)])


def shards(positions, recip, moire_coef, counts, w_first, w_second, w_heads):
    electrons, slots, walkers = positions.shape[1:]
    features, states, hidden = w_first.shape
    rows = slots * walkers
    groups, shares = lax.axis_size(("x", "core")), lax.axis_size(("y", "z"))
    spread = 0.75 / slots
    total = 4 * (BASIS + hidden)
    work = 2 * states * rows * hidden * hidden
    args = (positions, recip, moire_coef[None], counts[None], w_first, w_second, w_heads)
    send, potential, basis, first, second, weights, select, w_two, w_heads_t = call(
        forward_kernel,
        [((4 * slots, walkers), F32), ((slots, walkers), F32), ((BASIS, rows), BF16),
         ((states, hidden, rows), F32), ((states, hidden, rows), F32), ((1, walkers), F32),
         ((features, 3 * BASIS), BF16), ((states, hidden, hidden), BF16), ((states, hidden, 16), BF16)],
        [(a.shape, a.dtype) for a in args] + [pltpu.SemaphoreType.DMA((len(args),))]
        + [((4, electrons, slots, walkers), F32), ((slots * BASIS, walkers), F32),
           ((states, hidden, 3 * BASIS), BF16), ((states, hidden, hidden), BF16), ((3 * BASIS, rows), BF16)],
        40, args, 2 * work, hbm=True)
    near = [send] + [along("x", send, k) for k in range(1, XS)]
    others = [along("core", block, 1) for block in near]

    def energy_body(*refs):
        energy_kernel(spread, *refs)

    def backward_body(*refs):
        backward_kernel(spread, *refs)

    message, sums, d_amp, d_hps = call(
        energy_body,
        [((shares, 1, walkers), F32), ((8, walkers), F32), ((states, slots, walkers), F32),
         ((states, slots, walkers), F32)],
        [((groups * 4 * slots, walkers), F32), ((slots, slots, walkers), F32)],
        4, (*near, *others, potential, weights), 1 << 20)
    messages = lax.all_to_all(message, ("y", "z"), 0, 0, tiled=True)
    part = total // YS
    size = part // ZS
    parts = call(
        backward_body,
        [((part, 128), F32)] * YS,
        [((total, 128), F32), ((states, 16, rows), F32)],
        20, (messages, d_amp, d_hps, sums, send, potential, basis, first, second, w_two, w_heads_t), 3 * work)
    parts = [parts[0]] + [along("y", parts[k], k) for k in range(1, YS)]
    line, = call(line_kernel, [((part, 128), F32)], [], 4, parts, 1 << 20)
    lines = lax.all_to_all(line.reshape(ZS, size, 128), "z", 0, 0, tiled=True)
    pieces, = call(piece_kernel, [((ZS, size, 128), F32)], [], 4, (lines,), 1 << 20)
    summed = lax.all_to_all(pieces, "z", 0, 0, tiled=True).reshape(part, 128)
    parts = [summed] + [along("y", summed, k) for k in range(1, YS)]
    energy_matrix, *grads = call(
        expand_kernel,
        [((slots, slots), F32)] + [((4 * w.shape[0], 128), F32) for w in (w_first, w_second, w_heads)],
        [((total, 128), F32)], 8, (*parts, select), 1 << 20)
    grads = [g.reshape(-1, hidden // 128, states, 128).transpose(0, 2, 1, 3).reshape(-1, states, hidden) for g in grads]
    return (energy_matrix, *grads)


def solution(mesh):
    mesh = Mesh(mesh.devices.reshape(XS, 2, YS, ZS), ("x", "core", "y", "z"))
    state, walker = ("x", "core"), ("y", "z")
    in_specs = (
        P(None, None, None, walker),
        P(),
        P(),
        P(walker),
        P(None, state, None),
        P(None, state, None),
        P(None, state, None),
    )
    out_specs = (P(), P(None, state, None), P(None, state, None), P(None, state, None))
    return jax.shard_map(shards, mesh=mesh, in_specs=in_specs, out_specs=out_specs, check_vma=False)
```
